128 devices in a mesh: fsdp: 32 (over z, x_hi, y), tp: 4 (over x_lo, core).
Axes of the slice: x: 4 (x_hi: 2, x_lo: 2; x = x_hi * 2 + x_lo), y: 4, z: 4, core: 2. Of those that a mesh axis runs over, the one named last changes fastest.
Arguments:
- tokens: bfloat16 [16384, 2048], P(('fsdp', 'tp')), may hold values from -6 to 6
- g_attn: bfloat16 [2048], P('fsdp'), may hold values from 0.5 to 1.5
- query_matrix: bfloat16 [2048, 2048], P('fsdp', 'tp'), may hold values from -0.125 to 0.125
- key_matrix: bfloat16 [2048, 512], P('fsdp', 'tp'), may hold values from -0.125 to 0.125
- value_matrix: bfloat16 [2048, 512], P('fsdp', 'tp'), may hold values from -0.125 to 0.125
- w_out: bfloat16 [2048, 2048], P('fsdp', 'tp'), may hold values from -1 to 1
- g_ffn: bfloat16 [2048], P('fsdp'), may hold values from 0.5 to 1.5
- w_router: bfloat16 [2048, 64], P('fsdp'), may hold values from -0.09375 to 0.09375
- shared_gate: bfloat16 [2048, 2816], P('fsdp', 'tp'), may hold values from -0.125 to 0.125
- shared_up: bfloat16 [2048, 2816], P('fsdp', 'tp'), may hold values from -0.125 to 0.125
- shared_down: bfloat16 [2048, 2816], P('fsdp', 'tp'), may hold values from -0.109375 to 0.109375
- expert_gate: bfloat16 [64, 2048, 1408], P('fsdp', None, 'tp'), may hold values from -0.125 to 0.125
- expert_up: bfloat16 [64, 2048, 1408], P('fsdp', None, 'tp'), may hold values from -0.125 to 0.125
- expert_down: bfloat16 [64, 2048, 1408], P('fsdp', None, 'tp'), may hold values from -0.15625 to 0.15625
- lengths: int32 [32, 3], P('fsdp'), may hold values from 1 to 510, as said below
- routes: int32 [16384, 2], P('fsdp'), may hold values from 0 to 63, all different within a row; in each aligned block of 512 rows (0 to 511, 512 to 1023, ...) at most 20 rows name the same one
- cotangent: bfloat16 [16384, 2048], P(('fsdp', 'tp')), may hold values from -6 to 6
Outputs:
- output: bfloat16 [16384, 2048], P(('fsdp', 'tp'))
- grad_tokens: bfloat16 [16384, 2048], P(('fsdp', 'tp'))
- grad_g_attn: float32 [2048], P('fsdp')
- grad_w_query: float32 [2048, 2048], P('fsdp', 'tp')
- grad_w_key: float32 [2048, 512], P('fsdp', 'tp')
- grad_w_value: float32 [2048, 512], P('fsdp', 'tp')
- grad_w_out: float32 [2048, 2048], P('fsdp', 'tp')
- grad_g_ffn: float32 [2048], P('fsdp')
- grad_w_router: float32 [2048, 64], P('fsdp')
- grad_shared_gate: float32 [2048, 2816], P('fsdp', 'tp')
- grad_shared_up: float32 [2048, 2816], P('fsdp', 'tp')
- grad_shared_down: float32 [2048, 2816], P('fsdp', 'tp')
- grad_expert_gate: float32 [64, 2048, 1408], P('fsdp', None, 'tp')
- grad_expert_up: float32 [64, 2048, 1408], P('fsdp', None, 'tp')
- grad_expert_down: float32 [64, 2048, 1408], P('fsdp', None, 'tp')
The draws below stay inside these ranges and needn't reach their ends.
Inputs may be any that keep to these rules, and one draw needn't show every extreme that they name: In each group of 512 tokens the 3 lengths sum to 512; one of them, in a place drawn from the seed, is longer than 384; in one group, drawn from the seed, the two others are 1 token each. `routes`: each token names 2 different experts; among the rows of one device (one group) no expert is named more than 20 times, a bound that some block reaches.
All inputs are finite; a program needn't handle non-finite values.
Results may differ from the reference program's by a relative error of at most 0.03.
Values may be sent and summed in bfloat16 or wider, within the bound.
No kernel may reach another device: no remote copies, remote signals or barrier semaphores. Data moves between devices by JAX's collectives and lax.ppermute only.
A program may use at most 256 MiB of HBM per device.

```python
import math
import jax
import jax.numpy as jnp
import numpy as np
from jax import lax

MODEL_DIM = 2048
QUERY_HEADS = 16
KEY_VALUE_HEADS = 4
HEAD_SIZE = 128
FF = 1408
FFS = 2816
TOK_DEV = 128
TOPK = 2
SEQS = 3
GROUP_TOKENS = 512
GROUPS = 32
TOKENS = 16384
EXPERTS = 64
CAP = 20


def draw_lengths(key, part):
    key = jax.random.fold_in(key, 7)
    key_first, key_second, key_place, key_group = jax.random.split(key, 4)
    first_len = jax.random.randint(key_first, (GROUPS,), 1, TOK_DEV // 2)
    second = jax.random.randint(key_second, (GROUPS,), 1, TOK_DEV // 2)
    short_group = jax.random.randint(key_group, (), 0, GROUPS)
    group_ids = jnp.arange(GROUPS, dtype=jnp.int32)
    first_len = jnp.where(group_ids == short_group, 1, first_len)
    second = jnp.where(group_ids == short_group, 1, second)
    longest = GROUP_TOKENS - first_len - second
    where_long = jax.random.randint(key_place, (GROUPS, 1), 0, SEQS)
    column = jnp.arange(SEQS, dtype=jnp.int32)[None, :]
    rank_of = column - (column > where_long).astype(jnp.int32)
    others = jnp.where(rank_of == 0, first_len[:, None], second[:, None])
    return jnp.where(column == where_long, longest[:, None], others).astype(jnp.int32)


def shard_levels(stream_key, shape, cuts, low, high):
    def one(axis_at, parts):
        heights = jax.random.uniform(jax.random.fold_in(jax.random.fold_in(stream_key, 6), axis_at), (parts,), jnp.float32, low / len(cuts), high / len(cuts))
        return jnp.repeat(jnp.exp(heights), shape[axis_at] // parts).reshape((-1,) + (1,) * (len(shape) - axis_at - 1))

    level = one(*cuts[0])
    for cut in cuts[1:]:
        level = level * one(*cut)
    return level


def routed_block(own_key, own, number, rows, amount, top, reach, lean):
    ranking = jax.random.permutation(own_key, amount)
    heavy_load, common = portions_of(amount, rows * top, reach, lean, True), portions_of(amount, rows * top, reach, lean, False)
    places = jnp.arange(amount)

    def named(sizes, rotation):
        used = int((sizes > 0).sum())
        fixed = max(1, used // 4)
        shifted = fixed + (places - fixed + rotation * (used - fixed)) % max(1, amount - fixed)
        return jnp.zeros((amount,), jnp.int32).at[ranking[jnp.where(places < fixed, places, shifted)]].set(jnp.asarray(sizes, jnp.int32))

    sizes = jnp.where(number % 4 == 0, named(heavy_load, number // 4), named(common, number - number // 4 - 1))
    mixed = jax.random.permutation(jax.random.fold_in(own, 3), amount)
    giver, sink = mixed[0:amount // 2 * 2:2], mixed[1:amount // 2 * 2:2]
    margin = jnp.minimum(sizes[giver] - 1, reach - sizes[sink]) // 2
    margin = jnp.where((giver == ranking[0]) | (sink == ranking[0]) | (sizes[sink] == 0), 0, jnp.maximum(margin, 0))
    shifted = jax.random.randint(jax.random.fold_in(own, 4), (amount // 2,), 0, 1 << 20) % (margin + 1)
    sizes = sizes.at[giver].add(-shifted).at[sink].add(shifted)
    items = jnp.searchsorted(jnp.cumsum(sizes), jnp.arange(rows * top), side="right").astype(jnp.int32)
    grid = items.reshape(top, rows).T
    grid = grid[jax.random.permutation(jax.random.fold_in(own, 1), rows)]
    rotation = jax.random.randint(jax.random.fold_in(own, 2), (rows, 1), 0, top)
    return jnp.take_along_axis(grid, (jnp.arange(top)[None, :] + rotation) % top, axis=1)


def portions_of(count, total, limit, lean, full):
    portions = [(1 << 20) // math.isqrt(standing ** lean) + 1 for standing in range(1, count + 1)]
    largest = limit if full else min(limit, max(-(-total // count), total * portions[0] // sum(portions)))
    least = 1 if total - largest >= count - 1 else 0
    given, rest = [largest] + [least] * (count - 1), total - largest - least * (count - 1)
    while rest > 0:
        free = [i for i in range(1, count) if given[i] < largest] or [i for i in range(1, count) if given[i] < limit]
        mass, left = sum([portions[i] for i in free]), rest
        for i in free:
            addition = min(limit - given[i], max(1, left * portions[i] // mass), rest)
            given[i] = given[i] + addition
            rest = rest - addition
    return np.array(given)


def bell_draw(rng, shape, scale, limit, cuts=(), held_as=jnp.bfloat16):
    loudness = shard_levels(rng, shape, cuts, -0.22, 0.18) if cuts else 1.0
    result = jax.random.normal(rng, shape, jnp.float32) * scale * loudness
    return jnp.minimum(jnp.maximum(result, -limit), limit).astype(held_as)


def setup_inputs(seed: int = 0) -> dict:
    key_list = jax.random.split(jax.random.key(seed), 18)
    tokens = bell_draw(key_list[0], (TOKENS, MODEL_DIM), 1.0, 6.0, ((0, 128),))
    g_attn = jnp.clip(1.0 + 0.1 * jax.random.normal(key_list[1], (MODEL_DIM,), jnp.float32), 0.5, 1.5).astype(jnp.bfloat16)
    query_matrix = bell_draw(key_list[2], (MODEL_DIM, QUERY_HEADS * HEAD_SIZE), MODEL_DIM ** -0.5, 0.125, ((0, 32), (1, 4)))
    key_matrix = bell_draw(key_list[3], (MODEL_DIM, KEY_VALUE_HEADS * HEAD_SIZE), MODEL_DIM ** -0.5, 0.125, ((0, 32), (1, 4)))
    value_matrix = bell_draw(key_list[4], (MODEL_DIM, KEY_VALUE_HEADS * HEAD_SIZE), MODEL_DIM ** -0.5, 0.125, ((0, 32), (1, 4)))
    w_out = bell_draw(key_list[5], (MODEL_DIM, QUERY_HEADS * HEAD_SIZE), (QUERY_HEADS * HEAD_SIZE // 64) ** -0.5, 1.0, ((0, 32), (1, 4)))
    g_ffn = jnp.clip(1.0 + 0.1 * jax.random.normal(key_list[6], (MODEL_DIM,), jnp.float32), 0.5, 1.5).astype(jnp.bfloat16)
    w_router = bell_draw(key_list[7], (MODEL_DIM, EXPERTS), (MODEL_DIM * 16 // 9) ** -0.5, 0.09375, ((0, 32),))
    shared_gate = bell_draw(key_list[8], (MODEL_DIM, FFS), MODEL_DIM ** -0.5, 0.125, ((0, 32), (1, 4)))
    shared_up = bell_draw(key_list[9], (MODEL_DIM, FFS), MODEL_DIM ** -0.5, 0.125, ((0, 32), (1, 4)))
    shared_down = bell_draw(key_list[10], (MODEL_DIM, FFS), FFS ** -0.5, 0.109375, ((0, 32), (1, 4)))
    expert_gate = bell_draw(key_list[11], (EXPERTS, MODEL_DIM, FF), MODEL_DIM ** -0.5, 0.125, ((0, 32), (2, 4)))
    expert_up = bell_draw(key_list[12], (EXPERTS, MODEL_DIM, FF), MODEL_DIM ** -0.5, 0.125, ((0, 32), (2, 4)))
    expert_down = bell_draw(key_list[13], (EXPERTS, MODEL_DIM, FF), FF ** -0.5, 0.15625, ((0, 32), (2, 4)))
    lengths = draw_lengths(jax.random.fold_in(key_list[17], 71), 0)
    routes_keys = jax.random.split(jax.random.fold_in(key_list[15], 1), TOKENS // GROUP_TOKENS)
    routes_turns = jax.random.permutation(jax.random.fold_in(key_list[15], 3), TOKENS // GROUP_TOKENS)
    routes = jax.vmap(lambda own, number: routed_block(jax.random.fold_in(key_list[15], 2), own, number, GROUP_TOKENS, EXPERTS, TOPK, CAP, 1))(routes_keys, routes_turns).reshape((TOKENS, TOPK))
    cotangent = bell_draw(key_list[16], (TOKENS, MODEL_DIM), 1.0, 6.0, ((0, 128),))
    return {"tokens": tokens, "g_attn": g_attn, "query_matrix": query_matrix, "key_matrix": key_matrix, "value_matrix": value_matrix, "w_out": w_out, "g_ffn": g_ffn, "w_router": w_router, "shared_gate": shared_gate, "shared_up": shared_up, "shared_down": shared_down, "expert_gate": expert_gate, "expert_up": expert_up, "expert_down": expert_down, "lengths": lengths, "routes": routes, "cotangent": cotangent}


@jax.custom_vjp
def low(v):
    return lax.optimization_barrier(v.astype(jnp.bfloat16)).astype(jnp.float32)

@jax.custom_vjp
def low_back(v):
    return v

def low_keep(v):
    return (low(v), None)

def low_pass(kept, grad):
    return (grad,)

def back_keep(v):
    return (v, None)

def back_low(kept, grad):
    return (low(grad),)
low.defvjp(low_keep, low_pass)
low_back.defvjp(back_keep, back_low)
epsilon = 1e-06
highest = lax.Precision.HIGHEST

def rounded_rows(values):
    return low(low_back(values))

def matmul_result(left_op, right_op):
    return jnp.dot(left_op, right_op, precision=highest)

def product_t(left_op, right_op):
    return lax.dot_general(left_op, right_op, (((1,), (1,)), ((), ())), precision=highest)

def rms_norm(values, gain_vec):
    return values * lax.rsqrt(lax.optimization_barrier(jnp.mean(values * values, axis=-1, keepdims=True)) + epsilon) * gain_vec

def sequence_ids(seq_lens, row_count):
    seq_ends = jnp.cumsum(seq_lens)
    places = jnp.arange(row_count, dtype=jnp.int32)
    return lax.optimization_barrier(jnp.sum((places[:, None] >= seq_ends[None, :]).astype(jnp.int32), axis=1))

def route_tables(routes):
    flat_routes = routes.reshape(GROUPS, GROUP_TOKENS * TOPK)
    hot_table = (flat_routes[:, :, None] == jnp.arange(EXPERTS, dtype=jnp.int32)[None, None, :]).astype(jnp.int32)
    earlier = jnp.cumsum(hot_table, axis=1) - hot_table
    slot_of = lax.optimization_barrier(jnp.sum(earlier * hot_table, axis=2))
    group_base = jnp.arange(GROUPS, dtype=jnp.int32)[:, None] * CAP
    target = (flat_routes * (GROUPS * CAP) + group_base + slot_of).reshape(TOKENS * TOPK).astype(jnp.int32)
    owners = jnp.arange(TOKENS * TOPK, dtype=jnp.int32) // TOPK
    source_row = jnp.zeros((EXPERTS * GROUPS * CAP,), jnp.int32).at[target].set(owners)
    filled = jnp.zeros((EXPERTS * GROUPS * CAP,), jnp.float32).at[target].set(1.0)
    return (target.reshape(TOKENS, TOPK), source_row.reshape(EXPERTS, GROUPS * CAP), filled.reshape(EXPERTS, GROUPS * CAP))

def attend_group(normalized_rows, query_matrix, key_matrix, value_matrix, seq_lens):
    repeat_factor = QUERY_HEADS // KEY_VALUE_HEADS
    query_rows = rounded_rows(matmul_result(normalized_rows, query_matrix)).reshape(GROUP_TOKENS, KEY_VALUE_HEADS, repeat_factor, HEAD_SIZE)
    key_vectors = rounded_rows(matmul_result(normalized_rows, key_matrix)).reshape(GROUP_TOKENS, KEY_VALUE_HEADS, HEAD_SIZE)
    value_vectors = rounded_rows(matmul_result(normalized_rows, value_matrix)).reshape(GROUP_TOKENS, KEY_VALUE_HEADS, HEAD_SIZE)
    seq_of = sequence_ids(seq_lens, GROUP_TOKENS)
    places = jnp.arange(GROUP_TOKENS, dtype=jnp.int32)
    visible = (seq_of[:, None] == seq_of[None, :]) & (places[None, :] <= places[:, None])
    scores = low_back(jnp.einsum('qgrd,kgd->grqk', query_rows, key_vectors, precision=highest) * HEAD_SIZE ** (-0.5))
    scores = jnp.where(visible[None, None], scores, -1e+30)
    probability = jax.nn.softmax(scores, axis=-1)
    attended = jnp.einsum('grqk,kgd->qgrd', low(probability), value_vectors, precision=highest)
    return rounded_rows(attended.reshape(GROUP_TOKENS, QUERY_HEADS * HEAD_SIZE))

def layer(tokens, g_attn, query_matrix, key_matrix, value_matrix, w_out, g_ffn, w_router, shared_gate, shared_up, shared_down, expert_gate, expert_up, expert_down, lengths, routes, target, source_row, filled):
    h_attn = low(rms_norm(tokens, g_attn))

    def group_step(state_in, inputs):
        return (state_in, attend_group(inputs[0], query_matrix, key_matrix, value_matrix, inputs[1]))
    checked = jax.checkpoint(group_step)
    attended = lax.scan(checked, jnp.zeros((), jnp.float32), (h_attn.reshape(GROUPS, GROUP_TOKENS, MODEL_DIM), lengths))[1]
    attended = attended.reshape(TOKENS, QUERY_HEADS * HEAD_SIZE)
    middle = tokens + low_back(product_t(attended, w_out))
    h_ffn = low(rms_norm(middle, g_ffn))
    logits = low_back(matmul_result(h_ffn, w_router))
    chosen = jnp.take_along_axis(logits, routes, axis=1)
    gate_vals = jax.nn.softmax(chosen, axis=-1)

    def run_expert(inputs):
        gate_w, up_w, down_w, row_index, alive = inputs
        picked = h_ffn[row_index] * alive[:, None]
        gate_pre = low_back(matmul_result(picked, gate_w))
        up_pre = low_back(matmul_result(picked, up_w))
        hidden = low(jax.nn.silu(gate_pre) * up_pre)
        return low_back(product_t(hidden, down_w))
    expert_rows = lax.map(jax.checkpoint(run_expert), (expert_gate, expert_up, expert_down, source_row, filled))
    flat_rows = expert_rows.reshape(EXPERTS * GROUPS * CAP, MODEL_DIM)
    routed = lax.optimization_barrier(jnp.sum(gate_vals[:, :, None] * flat_rows[target], axis=1))
    s_gate_pre = low_back(matmul_result(h_ffn, shared_gate))
    s_up_pre = low_back(matmul_result(h_ffn, shared_up))
    s_hidden = low(jax.nn.silu(s_gate_pre) * s_up_pre)
    shared_out = low_back(product_t(s_hidden, shared_down))
    return middle + routed + shared_out

def reference(tokens, g_attn, query_matrix, key_matrix, value_matrix, w_out, g_ffn, w_router, shared_gate, shared_up, shared_down, expert_gate, expert_up, expert_down, lengths, routes, cotangent):
    target, source_row, filled = route_tables(routes)
    primals = tuple((array_in.astype(jnp.float32) for array_in in (tokens, g_attn, query_matrix, key_matrix, value_matrix, w_out, g_ffn, w_router, shared_gate, shared_up, shared_down, expert_gate, expert_up, expert_down)))

    def forward(*arrays):
        return layer(*arrays, lengths, routes, target, source_row, filled)
    output, pullback = jax.vjp(forward, *primals)
    gradients = pullback(cotangent.astype(jnp.float32))
    return (output.astype(jnp.bfloat16), gradients[0].astype(jnp.bfloat16), gradients[1], gradients[2], gradients[3], gradients[4], gradients[5], gradients[6], gradients[7], gradients[8], gradients[9], gradients[10], gradients[11], gradients[12], gradients[13])
```

```python
import functools

import jax
import jax.numpy as jnp
from jax import lax
from jax.experimental import pallas as pl
from jax.experimental.pallas import tpu as pltpu
from jax.sharding import PartitionSpec as P

HEAD_SIZE = 128
NZ, NX, NY = 4, 2, 4
FSDP = NZ * NX * NY
TP = 4
CAP = 20
LANES = 128
BLOCK_ORDER = (0, 2, 1, 3)
bf16 = jnp.bfloat16
f32 = jnp.float32

epsilon = 1e-06


def contract_first(left_op, right_op):
    return lax.dot_general(
        left_op, right_op, (((0,), (0,)), ((), ())), preferred_element_type=f32
    )


def contract_last(left_op, right_op):
    return lax.dot_general(
        left_op, right_op, (((1,), (1,)), ((), ())), preferred_element_type=f32
    )


def matmul(left_op, right_op):
    return jnp.dot(left_op, right_op, preferred_element_type=f32)


def silu_slope(values):
    sigmoid_v = jax.nn.sigmoid(values)
    return sigmoid_v * (1.0 + values * (1.0 - sigmoid_v))


def norm_rows(values, gain_vec):
    factor = lax.rsqrt(jnp.mean(values * values, axis=-1, keepdims=True) + epsilon)
    return (values * factor * gain_vec, factor)


def norm_back(values, factor, gain_vec, upstream):
    scaled_up = upstream * gain_vec
    return factor * scaled_up - values * factor * factor * factor * jnp.mean(
        scaled_up * values, axis=-1, keepdims=True
    )


def move_fsdp(values, dz, dx, dy):
    pairs = []
    for z in range(NZ):
        for x in range(NX):
            for y in range(NY):
                target = (((z + dz) % NZ) * NX + (x + dx) % NX) * NY + (y + dy) % NY
                pairs.append(((z * NX + x) * NY + y, target))
    return lax.ppermute(values, "fsdp", pairs)


def move_tp(values, flip):
    return lax.ppermute(values, "tp", [(i, i ^ flip) for i in range(TP)])


def gather_tp(own):
    pair = jnp.concatenate([own, move_tp(own, 2)], axis=0)
    return jnp.concatenate([pair, move_tp(pair, 1)], axis=0)


def scatter_tp(near_part, far_part):
    summed = near_part + move_tp(far_part.astype(bf16), 1).astype(f32)
    rows = summed.shape[0] // 2
    return summed[:rows] + move_tp(summed[rows:].astype(bf16), 2).astype(f32)


def small_sum_tp(values):
    return values + move_tp(values, 1) + move_tp(values, 2) + move_tp(values, 3)


def swap_fsdp(values):
    shape = values.shape
    blocks = values.reshape(FSDP, shape[0] // FSDP, shape[1])
    return lax.all_to_all(blocks, "fsdp", split_axis=0, concat_axis=0, tiled=True).reshape(shape)


def place_kernel(cuts, spot, *refs):
    first, second = refs[:NZ], refs[NZ : NZ + NY]
    outs = refs[NZ + NY :]
    z, x, y = spot[0], spot[1], spot[2]
    half = first[0].shape[3]
    for zr in range(NZ):
        for xr in range(NX):
            for yr in range(NY):
                at = (lax.rem(z + zr, NZ), lax.rem(x + xr, NX), lax.rem(y + yr, NY))
                for number, (item, start, width) in enumerate(cuts):
                    columns = slice(start, start + width)
                    outs[number][at[0], at[1], at[2], :half] = first[zr][yr, xr, item, :, columns]
                    outs[number][at[0], at[1], at[2], half:] = second[yr][zr, xr, item, :, columns]


def gather_fsdp(stacked, spot, cuts):
    items, rows, columns = stacked.shape
    half = rows // 2
    pair = jnp.stack([stacked, move_fsdp(stacked, 0, 1, 0)])
    near_y, near_z = pair[:, :, :half], pair[:, :, half:]
    by_y = jnp.stack([near_y] + [move_fsdp(near_y, 0, 0, -r) for r in range(1, NY)])
    by_z = jnp.stack([near_z] + [move_fsdp(near_z, -r, 0, 0) for r in range(1, NZ)])
    first = [by_y] + [move_fsdp(by_y, -r, 0, 0) for r in range(1, NZ)]
    second = [by_z] + [move_fsdp(by_z, 0, 0, -r) for r in range(1, NY)]
    total = FSDP * rows
    wholes = pl.pallas_call(
        functools.partial(place_kernel, cuts),
        out_shape=[jax.ShapeDtypeStruct((NZ, NX, NY, rows, width), bf16) for _, _, width in cuts],
        in_specs=[pl.BlockSpec(memory_space=pltpu.SMEM)]
        + [pl.BlockSpec(memory_space=pltpu.VMEM)] * (NZ + NY),
        out_specs=[pl.BlockSpec(memory_space=pltpu.VMEM)] * len(cuts),
        compiler_params=pltpu.CompilerParams(vmem_limit_bytes=32 * 1024 * 1024),
        cost_estimate=pl.CostEstimate(
            flops=0, bytes_accessed=4 * total * sum(w for _, _, w in cuts), transcendentals=0
        ),
        name="place",
    )(spot, *first, *second)
    return [whole.reshape(total, width) for whole, (_, _, width) in zip(wholes, cuts)]


def pick(values, index, axis):
    return lax.dynamic_index_in_dim(values, index, axis, keepdims=False)


def scatter_fsdp(join, grads, spot):
    z, x, y = spot[0], spot[1], spot[2]
    rows = grads[0].shape[0] // FSDP
    views = [g.reshape(NZ, NX, NY, 2, rows // 2, g.shape[1]) for g in grads]
    joined = lambda parts: join([p[None] for p in parts])

    def first_sum(cut, count, send):
        total = cut(0).astype(f32)
        for r in range(1, count):
            total = total + send(cut(r), r).astype(f32)
        return total.astype(bf16)

    def last_sum(kept):
        mine, theirs = pick(kept, x, 1), pick(kept, 1 - x, 1)
        return mine.astype(f32) + move_fsdp(theirs, 0, 1, 0).astype(f32)

    def send_z(part, r):
        return move_fsdp(part, r, 0, 0)

    def send_y(part, r):
        return move_fsdp(part, 0, 0, r)

    def z_index(r):
        return lax.rem(z + r, NZ)

    def y_index(r):
        return lax.rem(y + r, NY)

    one = first_sum(lambda r: joined([pick(v, z_index(r), 0)[:, :, 0] for v in views]), NZ, send_z)
    two = first_sum(
        lambda r: joined([pick(v, y_index(r), 2)[:, :, 1] for v in views]), NY, send_y
    )
    one = first_sum(lambda r: pick(one, y_index(r), 2), NY, send_y)
    two = first_sum(lambda r: pick(two, z_index(r), 1), NZ, send_z)
    return jnp.concatenate([last_sum(one), last_sum(two)], axis=1)


def fill_bias(where, bias):
    size = bias.shape[0]
    rank, end_one, end_two = where[0], where[1], where[2]

    def place_of(index):
        block = lax.div(index, LANES)
        block = 2 * lax.rem(block, 2) + lax.div(block, 2)
        return jnp.bitwise_xor(block, rank) * LANES + lax.rem(index, LANES)

    queries = place_of(lax.broadcasted_iota(jnp.int32, (size, 1), 0))
    keys = place_of(lax.broadcasted_iota(jnp.int32, (1, size), 1))
    start = jnp.where(queries >= end_two, end_two, jnp.where(queries >= end_one, end_one, 0))
    visible = (keys <= queries) & (keys >= start)
    bias[...] = jnp.where(visible, 0.0, -1e30).astype(f32)


def exponents(q_ref, k_ref, bias):
    scores = contract_last(q_ref[...], k_ref[...]) * (HEAD_SIZE**-0.5) + bias[...]
    exponent = jnp.exp(scores - jnp.max(scores, axis=-1, keepdims=True))
    return exponent / jnp.sum(exponent, axis=-1, keepdims=True)


def attend_kernel(where, q_ref, k_ref, v_ref, out_ref, bias):
    @pl.when(pl.program_id(0) == 0)
    def _():
        fill_bias(where, bias)

    probability = exponents(q_ref, k_ref, bias).astype(bf16)
    out_ref[...] = matmul(probability, v_ref[...]).astype(bf16)


def attend(where, qkv, heads):
    rows = qkv.shape[0]
    block = (rows, HEAD_SIZE)
    return pl.pallas_call(
        attend_kernel,
        out_shape=jax.ShapeDtypeStruct((rows, heads * HEAD_SIZE), bf16),
        grid_spec=pltpu.PrefetchScalarGridSpec(
            num_scalar_prefetch=1,
            grid=(heads,),
            in_specs=[
                pl.BlockSpec(block, lambda h, w: (0, h)),
                pl.BlockSpec(block, lambda h, w: (0, heads)),
                pl.BlockSpec(block, lambda h, w: (0, heads + 1)),
            ],
            out_specs=pl.BlockSpec(block, lambda h, w: (0, h)),
            scratch_shapes=[pltpu.VMEM((rows, rows), f32)],
        ),
        compiler_params=pltpu.CompilerParams(vmem_limit_bytes=40 * 1024 * 1024),
        cost_estimate=pl.CostEstimate(
            flops=4 * heads * rows * rows * HEAD_SIZE,
            bytes_accessed=4 * rows * heads * HEAD_SIZE,
            transcendentals=heads * rows * rows,
        ),
        name="attend",
    )(where, qkv, qkv, qkv)


def attend_back_kernel(heads, where, q_ref, k_ref, v_ref, g_ref, out_ref, bias, key_sum, value_sum):
    head = pl.program_id(0)

    @pl.when(head == 0)
    def _():
        fill_bias(where, bias)
        key_sum[...] = jnp.zeros_like(key_sum)
        value_sum[...] = jnp.zeros_like(value_sum)

    scale = HEAD_SIZE**-0.5
    probability = exponents(q_ref, k_ref, bias)
    grad_prob = contract_last(g_ref[...], v_ref[...])
    inner = jnp.sum(probability * grad_prob, axis=-1, keepdims=True)
    grad_scores = (probability * (grad_prob - inner)).astype(bf16)
    columns = pl.ds(pl.multiple_of(head * HEAD_SIZE, HEAD_SIZE), HEAD_SIZE)
    out_ref[:, columns] = (matmul(grad_scores, k_ref[...]) * scale).astype(bf16)
    key_sum[...] += contract_first(grad_scores, q_ref[...])
    value_sum[...] += contract_first(probability.astype(bf16), g_ref[...])

    @pl.when(head == heads - 1)
    def _():
        wide = heads * HEAD_SIZE
        out_ref[:, wide : wide + HEAD_SIZE] = (key_sum[...] * scale).astype(bf16)
        out_ref[:, wide + HEAD_SIZE :] = value_sum[...].astype(bf16)


def attend_back(where, qkv, grads, heads):
    rows = qkv.shape[0]
    block = (rows, HEAD_SIZE)
    return pl.pallas_call(
        functools.partial(attend_back_kernel, heads),
        out_shape=jax.ShapeDtypeStruct(qkv.shape, bf16),
        grid_spec=pltpu.PrefetchScalarGridSpec(
            num_scalar_prefetch=1,
            grid=(heads,),
            in_specs=[
                pl.BlockSpec(block, lambda h, w: (0, h)),
                pl.BlockSpec(block, lambda h, w: (0, heads)),
                pl.BlockSpec(block, lambda h, w: (0, heads + 1)),
                pl.BlockSpec(block, lambda h, w: (0, h)),
            ],
            out_specs=pl.BlockSpec(qkv.shape, lambda h, w: (0, 0)),
            scratch_shapes=[
                pltpu.VMEM((rows, rows), f32),
                pltpu.VMEM(block, f32),
                pltpu.VMEM(block, f32),
            ],
        ),
        compiler_params=pltpu.CompilerParams(vmem_limit_bytes=40 * 1024 * 1024),
        cost_estimate=pl.CostEstimate(
            flops=10 * heads * rows * rows * HEAD_SIZE,
            bytes_accessed=6 * rows * heads * HEAD_SIZE,
            transcendentals=heads * rows * rows,
        ),
        name="attend_back",
    )(where, qkv, qkv, qkv, grads)


def expert_grads_kernel(core, rows_own, rows_far, grads_own, grads_far, d_gate, d_up, scaled, *outs):
    half = pl.program_id(0)

    def write(rows, grads):
        outs[0][...] = contract_first(d_gate[...], rows[...])
        outs[1][...] = contract_first(d_up[...], rows[...])
        outs[2][...] = contract_first(scaled[...], grads[...])

    pl.when(half == 0)(lambda: write(rows_own, grads_own))
    pl.when(half == 1)(lambda: write(rows_far, grads_far))


def expert_grads(core, rows_own, rows_far, grads_own, grads_far, d_gate, d_up, scaled):
    rows, wide = rows_own.shape
    hidden = d_gate.shape[1]
    full = pl.BlockSpec((rows, wide), lambda h, c: (0, 0))
    part = pl.BlockSpec((rows, hidden), lambda h, c: (0, 0))
    result = pl.BlockSpec((hidden, wide), lambda h, c: (0, jnp.bitwise_xor(h, c[0])))
    return pl.pallas_call(
        expert_grads_kernel,
        out_shape=[jax.ShapeDtypeStruct((hidden, 2 * wide), f32)] * 3,
        grid_spec=pltpu.PrefetchScalarGridSpec(
            num_scalar_prefetch=1,
            grid=(2,),
            in_specs=[full] * 4 + [part] * 3,
            out_specs=[result] * 3,
        ),
        compiler_params=pltpu.CompilerParams(vmem_limit_bytes=56 * 1024 * 1024),
        cost_estimate=pl.CostEstimate(
            flops=12 * rows * wide * hidden,
            bytes_accessed=24 * hidden * wide + 12 * rows * wide,
            transcendentals=0,
        ),
        name="expert_grads",
    )(core, rows_own, rows_far, grads_own, grads_far, d_gate, d_up, scaled)


def per_device(
    tokens,
    g_attn,
    query_matrix,
    key_matrix,
    value_matrix,
    w_out,
    g_ffn,
    w_router,
    shared_gate,
    shared_up,
    shared_down,
    expert_gate,
    expert_up,
    expert_down,
    lengths,
    routes,
    cotangent,
):
    tok_dev, dim = tokens.shape
    group_rows = tok_dev * TP
    near = group_rows // 2
    experts = w_router.shape[1]
    own_rows = w_router.shape[0]
    q_width, kv_width = query_matrix.shape[1], key_matrix.shape[1]
    qkv_width = q_width + 2 * kv_width
    heads = q_width // HEAD_SIZE
    local_experts, _, hidden_own = expert_gate.shape
    half_dim = dim // 2
    fsdp_at = lax.axis_index("fsdp")
    rank = lax.axis_index("tp")
    core = lax.rem(rank, 2)
    core_vec = core.astype(jnp.int32).reshape(1)
    spot = jnp.stack(
        [fsdp_at // (NX * NY), lax.rem(fsdp_at // NY, NX), lax.rem(fsdp_at, NY)]
    ).astype(jnp.int32)

    small_tile = jnp.concatenate(
        [
            w_router,
            g_attn[:, None],
            g_ffn[:, None],
            jnp.zeros((own_rows, LANES - experts - 2), bf16),
        ],
        axis=1,
    )
    qkv_own = jnp.concatenate([query_matrix, key_matrix, value_matrix], axis=1)
    w_qkv, w_tile = gather_fsdp(
        jnp.concatenate([qkv_own, small_tile], axis=1)[None],
        spot,
        ((0, 0, qkv_width), (0, qkv_width, LANES)),
    )
    token_rows = gather_tp(tokens)
    grad_rows = gather_tp(cotangent)
    (w_out_all,) = gather_fsdp(w_out[None], spot, ((0, 0, q_width),))
    wide = shared_gate.shape[1]
    w_sgate, w_sup, w_sdown = gather_fsdp(
        jnp.stack([shared_gate, shared_up, shared_down]),
        spot,
        ((0, 0, wide), (1, 0, wide), (2, 0, wide)),
    )
    lane = lax.broadcasted_iota(jnp.int32, (8, LANES), 1)
    gain_pick = (lane == experts + lax.broadcasted_iota(jnp.int32, (8, LANES), 0)).astype(bf16)
    gains = contract_last(gain_pick, w_tile)
    gain_one, gain_two = gains[0:1], gains[1:2]

    route_blocks = routes.reshape(TP, tok_dev, routes.shape[1])
    own_routes = jnp.concatenate(
        [pick(route_blocks, jnp.bitwise_xor(b, rank), 0) for b in BLOCK_ORDER], axis=0
    )
    places = jnp.concatenate(
        [jnp.bitwise_xor(b, rank) * tok_dev + jnp.arange(tok_dev) for b in BLOCK_ORDER]
    ).astype(jnp.int32)
    expert_lane = jnp.arange(LANES, dtype=jnp.int32)[None, :]
    hot = (own_routes[:, 0:1] == expert_lane) | (own_routes[:, 1:2] == expert_lane)
    before = (places[None, :] < places[:, None]).astype(bf16)
    earlier = matmul(before, hot.astype(bf16))
    slots = experts * CAP
    slot_ids = jnp.arange(slots, dtype=jnp.int32)
    spread = (slot_ids[None, :] // CAP == jnp.arange(LANES, dtype=jnp.int32)[:, None]).astype(bf16)
    slot_wanted = matmul(jnp.where(hot, earlier, -1.0).astype(bf16), spread)
    dispatch = (slot_wanted == (slot_ids % CAP).astype(f32)[None, :]).astype(bf16)

    def core_half(values):
        return lax.dynamic_slice_in_dim(values, core * half_dim, half_dim, 1)

    slot_grads = contract_first(dispatch, core_half(grad_rows)).astype(bf16)
    grads_own = swap_fsdp(slot_grads)
    grads_far = move_tp(grads_own, 1)

    hidden_all = local_experts * hidden_own

    def expert_halves(weights):
        both = jnp.swapaxes(weights, 1, 2).reshape(hidden_all, dim)
        return core_half(both), lax.dynamic_slice_in_dim(both, (1 - core) * half_dim, half_dim, 1)

    eg_own, eg_far = expert_halves(expert_gate)
    eu_own, eu_far = expert_halves(expert_up)
    ed_own, ed_far = expert_halves(expert_down)

    ends = jnp.cumsum(lengths[0])
    where = jnp.stack([rank.astype(jnp.int32), ends[0], ends[1]]).astype(jnp.int32)
    normed_one, _ = norm_rows(token_rows.astype(f32), gain_one)
    h_attn = normed_one.astype(bf16)
    qkv = matmul(h_attn, w_qkv).astype(bf16)
    attended = attend(where, qkv, heads)
    attn_own = scatter_tp(
        contract_last(attended[:near], w_out_all), contract_last(attended[near:], w_out_all)
    )
    own_tokens = tokens.astype(f32)
    middle = own_tokens + attn_own
    normed_two, factor_two = norm_rows(middle, gain_two)
    h_ffn = gather_tp(normed_two.astype(bf16))

    slot_rows = contract_first(dispatch, core_half(h_ffn)).astype(bf16)
    rows_own = swap_fsdp(slot_rows)
    rows_far = move_tp(rows_own, 1)

    logits = matmul(h_ffn, w_tile)
    top = jnp.max(jnp.where(hot, logits, -1e30), axis=-1, keepdims=True)
    gate_exp = jnp.where(hot, jnp.exp(jnp.minimum(logits - top, 0.0)), 0.0)
    gates = gate_exp / jnp.sum(gate_exp, axis=-1, keepdims=True)
    gate_high = gates.astype(bf16)
    gate_low = (gates - gate_high.astype(f32)).astype(bf16)
    gate_lanes = jnp.concatenate([gate_high[:, :experts], gate_low[:, :experts]], axis=1)
    gated = (matmul(gate_high, spread) * dispatch.astype(f32)).astype(bf16)
    slot_gates = swap_fsdp(contract_first(dispatch, gate_lanes).astype(bf16))

    s_gate_pre = matmul(h_ffn, w_sgate)
    s_up_pre = matmul(h_ffn, w_sup)
    s_hidden = (jax.nn.silu(s_gate_pre) * s_up_pre).astype(bf16)
    grad_shidden = matmul(grad_rows, w_sdown)
    grad_sgate_pre = (grad_shidden * s_up_pre * silu_slope(s_gate_pre)).astype(bf16)
    grad_sup_pre = (grad_shidden * jax.nn.silu(s_gate_pre)).astype(bf16)
    grad_sdown = contract_first(grad_rows, s_hidden).astype(bf16)
    grad_sgate = contract_first(h_ffn, grad_sgate_pre).astype(bf16)
    grad_sup = contract_first(h_ffn, grad_sup_pre).astype(bf16)
    shared_sums = scatter_fsdp(
        lambda parts: jnp.concatenate(parts, axis=0), [grad_sgate, grad_sup, grad_sdown], spot
    )
    shared_out = contract_last(s_hidden, w_sdown)
    shared_back = contract_last(grad_sgate_pre, w_sgate) + contract_last(grad_sup_pre, w_sup)

    row_ids = lax.broadcasted_iota(jnp.int32, (slots, 1), 0)
    second = (row_ids % (local_experts * CAP)) // CAP
    mine = second == (lax.broadcasted_iota(jnp.int32, (1, hidden_all), 1) // hidden_own)

    gate_pre = contract_last(rows_own, eg_own) + contract_last(rows_far, eg_far)
    up_pre = contract_last(rows_own, eu_own) + contract_last(rows_far, eu_far)
    down_back = contract_last(grads_own, ed_own) + contract_last(grads_far, ed_far)
    silu_gate = jax.nn.silu(gate_pre)
    hidden_wide = jnp.where(mine, silu_gate * up_pre, 0.0)
    hidden = hidden_wide.astype(bf16)
    d_gate = jnp.where(mine, down_back * up_pre * silu_slope(gate_pre), 0.0).astype(bf16)
    d_up = jnp.where(mine, down_back * silu_gate, 0.0).astype(bf16)
    slot_dot = jnp.sum(hidden_wide * down_back, axis=1, keepdims=True)
    lane_ids = lax.broadcasted_iota(jnp.int32, (1, LANES), 1)
    expert_of = local_experts * fsdp_at.astype(jnp.int32) + second
    dot_high = slot_dot.astype(bf16)
    dot_low = (slot_dot - dot_high.astype(f32)).astype(bf16)
    zero = jnp.zeros((), bf16)
    dot_lanes = jnp.where(lane_ids == expert_of, dot_high, zero) + jnp.where(
        lane_ids == experts + expert_of, dot_low, zero
    )

    def back_product(gate_w, up_w):
        return matmul(d_gate, gate_w) + matmul(d_up, up_w)

    sent_far = move_tp(back_product(eg_far, eu_far).astype(bf16), 1)
    sent_own = (back_product(eg_own, eu_own) + sent_far.astype(f32)).astype(bf16)
    returned = swap_fsdp(jnp.concatenate([sent_own, dot_lanes], axis=1))

    out_far = move_tp(matmul(hidden, ed_far).astype(bf16), 1)
    out_own = (matmul(hidden, ed_own) + out_far.astype(f32)).astype(bf16)
    out_back = swap_fsdp(out_own)

    is_gate = (lane_ids == expert_of) | (lane_ids == experts + expert_of)
    gate_of = jnp.sum(jnp.where(is_gate, slot_gates.astype(f32), 0.0), axis=1, keepdims=True)
    grad_egate, grad_eup, grad_edown = expert_grads(
        core_vec,
        rows_own,
        rows_far,
        grads_own,
        grads_far,
        (gate_of * d_gate.astype(f32)).astype(bf16),
        (gate_of * d_up.astype(f32)).astype(bf16),
        (gate_of * hidden.astype(f32)).astype(bf16),
    )

    def expert_layout(grads):
        return jnp.swapaxes(grads.reshape(local_experts, hidden_own, dim), 1, 2)

    def whole_width(values):
        return jnp.concatenate(
            [jnp.where(core == 0, values, 0.0), jnp.where(core == 1, values, 0.0)], axis=1
        )

    routed = matmul(gated, out_back)
    out_part = shared_out + whole_width(routed)
    output = (middle + scatter_tp(out_part[:near], out_part[near:])).astype(bf16)

    combined = matmul(gated, returned)
    dots = combined[:, half_dim : half_dim + experts] + combined[:, half_dim + experts :]
    d_logits = dots - gates[:, :experts] * jnp.sum(dots, axis=-1, keepdims=True)
    d_logits = jnp.pad(d_logits.astype(bf16), ((0, 0), (0, LANES - experts)))
    ffn_part = (
        shared_back + whole_width(combined[:, :half_dim]) + contract_last(d_logits, w_tile)
    )
    d_h_ffn = scatter_tp(ffn_part[:near], ffn_part[near:])
    d_middle = cotangent.astype(f32) + norm_back(middle, factor_two, gain_two, d_h_ffn)
    gain_terms = (d_h_ffn * middle * factor_two).astype(bf16)
    gain_lane = jnp.broadcast_to(lane_ids == experts, (tok_dev, LANES)).astype(bf16)
    grad_tile = (contract_first(h_ffn, d_logits) + contract_first(gain_terms, gain_lane)).astype(
        bf16
    )
    d_att = gather_tp(d_middle.astype(bf16))
    grad_wout = contract_first(d_att, attended).astype(bf16)
    out_sums = scatter_fsdp(
        lambda parts: jnp.concatenate(parts, axis=-1), [grad_wout, grad_tile], spot
    )[0]
    tile_sums = small_sum_tp(out_sums[:, q_width:])

    d_attended = matmul(d_att, w_out_all).astype(bf16)
    d_qkv = attend_back(where, qkv, d_attended, heads)
    grad_wqkv = contract_first(h_attn, d_qkv).astype(bf16)
    qkv_sums = scatter_fsdp(lambda parts: parts[0], [grad_wqkv], spot)[0]
    d_h_attn = scatter_tp(
        contract_last(d_qkv[:near], w_qkv), contract_last(d_qkv[near:], w_qkv)
    )
    _, factor_one = norm_rows(own_tokens, gain_one)
    grad_tokens = (d_middle + norm_back(own_tokens, factor_one, gain_one, d_h_attn)).astype(bf16)
    gain_sum = jnp.sum(qkv_sums * qkv_own.astype(f32), axis=1)
    grad_g_attn = small_sum_tp(gain_sum) / g_attn.astype(f32)
    return (
        output,
        grad_tokens,
        grad_g_attn,
        qkv_sums[:, :q_width],
        qkv_sums[:, q_width : q_width + kv_width],
        qkv_sums[:, q_width + kv_width :],
        out_sums[:, :q_width],
        tile_sums[:, experts],
        tile_sums[:, :experts],
        shared_sums[0],
        shared_sums[1],
        shared_sums[2],
        expert_layout(grad_egate),
        expert_layout(grad_eup),
        expert_layout(grad_edown),
    )


def solution(mesh):
    in_specs = (
        P(("fsdp", "tp"), None),
        P("fsdp"),
        P("fsdp", "tp"),
        P("fsdp", "tp"),
        P("fsdp", "tp"),
        P("fsdp", "tp"),
        P("fsdp"),
        P("fsdp", None),
        P("fsdp", "tp"),
        P("fsdp", "tp"),
        P("fsdp", "tp"),
        P("fsdp", None, "tp"),
        P("fsdp", None, "tp"),
        P("fsdp", None, "tp"),
        P("fsdp", None),
        P("fsdp", None),
        P(("fsdp", "tp"), None),
    )
    out_specs = (
        P(("fsdp", "tp"), None),
        P(("fsdp", "tp"), None),
        P("fsdp"),
        P("fsdp", "tp"),
        P("fsdp", "tp"),
        P("fsdp", "tp"),
        P("fsdp", "tp"),
        P("fsdp"),
        P("fsdp", None),
        P("fsdp", "tp"),
        P("fsdp", "tp"),
        P("fsdp", "tp"),
        P("fsdp", None, "tp"),
        P("fsdp", None, "tp"),
        P("fsdp", None, "tp"),
    )
    return jax.shard_map(
        per_device, mesh=mesh, in_specs=in_specs, out_specs=out_specs, check_vma=False
    )
```

```python
import functools

import jax
import jax.numpy as jnp
from jax import lax
from jax.experimental import pallas as pl
from jax.experimental.pallas import tpu as pltpu
from jax.sharding import PartitionSpec as P

HEAD_SIZE = 128
NZ, NX, NY = 4, 2, 4
FSDP = NZ * NX * NY
TP = 4
CAP = 20
LANES = 128
BLOCK_ORDER = (0, 2, 1, 3)
bf16 = jnp.bfloat16
f32 = jnp.float32

epsilon = 1e-06


def contract_first(left_op, right_op):
    return lax.dot_general(
        left_op, right_op, (((0,), (0,)), ((), ())), preferred_element_type=f32
    )


def contract_last(left_op, right_op):
    return lax.dot_general(
        left_op, right_op, (((1,), (1,)), ((), ())), preferred_element_type=f32
    )


def matmul(left_op, right_op):
    return jnp.dot(left_op, right_op, preferred_element_type=f32)


def silu_slope(values):
    sigmoid_v = jax.nn.sigmoid(values)
    return sigmoid_v * (1.0 + values * (1.0 - sigmoid_v))


def norm_rows(values, gain_vec):
    factor = lax.rsqrt(jnp.mean(values * values, axis=-1, keepdims=True) + epsilon)
    return (values * factor * gain_vec, factor)


def norm_back(values, factor, gain_vec, upstream):
    scaled_up = upstream * gain_vec
    return factor * scaled_up - values * factor * factor * factor * jnp.mean(
        scaled_up * values, axis=-1, keepdims=True
    )


def after(value, *earlier):
    return lax.optimization_barrier((value, *earlier))[0]


def move_fsdp(values, dz, dx, dy):
    return route_fsdp(values, lambda z, x, y: ((z + dz) % NZ, (x + dx) % NX, (y + dy) % NY))


def swap_along(values, fz, fx, fy):
    return route_fsdp(values, lambda z, x, y: (z ^ fz, x ^ fx, y ^ fy))


def route_fsdp(values, target):
    pairs = []
    for z in range(NZ):
        for x in range(NX):
            for y in range(NY):
                to_z, to_x, to_y = target(z, x, y)
                pairs.append(((z * NX + x) * NY + y, (to_z * NX + to_x) * NY + to_y))
    return lax.ppermute(values, "fsdp", pairs)


def move_tp(values, flip):
    return lax.ppermute(values, "tp", [(i, i ^ flip) for i in range(TP)])


def gather_tp(own):
    pair = jnp.concatenate([own, move_tp(own, 2)], axis=0)
    return jnp.concatenate([pair, move_tp(pair, 1)], axis=0)


def scatter_tp(near_part, far_part):
    summed = near_part + move_tp(far_part.astype(bf16), 1).astype(f32)
    rows = summed.shape[0] // 2
    return summed[:rows] + move_tp(summed[rows:].astype(bf16), 2).astype(f32)


def small_sum_tp(values):
    return values + move_tp(values, 1) + move_tp(values, 2) + move_tp(values, 3)


def swap_fsdp(values):
    shape = values.shape
    blocks = values.reshape(FSDP, shape[0] // FSDP, shape[1])
    return lax.all_to_all(blocks, "fsdp", split_axis=0, concat_axis=0, tiled=True).reshape(shape)


def along(axis):
    grid = [[[(z * NX + x) * NY + y for y in range(NY)] for x in range(NX)] for z in range(NZ)]
    if axis == "z":
        return [[grid[z][x][y] for z in range(NZ)] for x in range(NX) for y in range(NY)]
    if axis == "x":
        return [[grid[z][x][y] for x in range(NX)] for z in range(NZ) for y in range(NY)]
    return [list(grid[z][x]) for z in range(NZ) for x in range(NX)]


def staged_sum(values):
    for axis in "zxy":
        values = lax.psum_scatter(
            values, "fsdp", scatter_dimension=0, tiled=True, axis_index_groups=along(axis)
        )
    return values


def place_kernel(cuts, spot, *refs):
    first, second, outs = refs[:5], refs[5:10], refs[10:]
    z, x, y = spot[0], spot[1], spot[2]
    half = first[0].shape[3]

    def part(pieces, across, along_line, xr, item, columns):
        if across == 2:
            across += along_line // 2
            along_line %= 2
        elif across == 3:
            across = 4
        return pieces[across][along_line, xr, item, :, columns]

    for zr in range(NZ):
        for xr in range(NX):
            for yr in range(NY):
                at = (jnp.bitwise_xor(z, zr), jnp.bitwise_xor(x, xr), jnp.bitwise_xor(y, yr))
                for number, (item, start, width) in enumerate(cuts):
                    columns = slice(start, start + width)
                    outs[number][at[0], at[1], at[2], :half] = part(
                        first, zr, yr, xr, item, columns
                    )
                    outs[number][at[0], at[1], at[2], half:] = part(
                        second, yr, zr, xr, item, columns
                    )


def gather_pair(stacked):
    half = stacked.shape[1] // 2
    pair = jnp.stack([stacked, swap_along(stacked, 0, 1, 0)])
    return pair[:, :, :half], pair[:, :, half:]


def gather_lines(pair):
    near_y, near_z = pair
    by_y = jnp.stack([near_y] + [swap_along(near_y, 0, 0, r) for r in range(1, NY)])
    by_z = jnp.stack([near_z] + [swap_along(near_z, r, 0, 0) for r in range(1, NZ)])
    return lax.optimization_barrier((by_y, by_z))


def gather_near(lines):
    by_y, by_z = lines
    return lax.optimization_barrier(
        (
            swap_along(by_y, 1, 0, 0),
            swap_along(by_y, 3, 0, 0),
            swap_along(by_z, 0, 0, 1),
            swap_along(by_z, 0, 0, 3),
        )
    )


def gather_all(lines, near, spot, cuts):
    by_y, by_z = lines
    rows = 2 * by_y.shape[3]
    first = [by_y, near[0], swap_along(near[0][:2], 3, 0, 0), swap_along(near[1][2:], 1, 0, 0), near[1]]
    second = [by_z, near[2], swap_along(near[2][:2], 0, 0, 3), swap_along(near[3][2:], 0, 0, 1), near[3]]
    total = FSDP * rows
    wholes = pl.pallas_call(
        functools.partial(place_kernel, cuts),
        out_shape=[jax.ShapeDtypeStruct((NZ, NX, NY, rows, width), bf16) for _, _, width in cuts],
        in_specs=[pl.BlockSpec(memory_space=pltpu.SMEM)]
        + [pl.BlockSpec(memory_space=pltpu.VMEM)] * 10,
        out_specs=[pl.BlockSpec(memory_space=pltpu.VMEM)] * len(cuts),
        compiler_params=pltpu.CompilerParams(vmem_limit_bytes=32 * 1024 * 1024),
        cost_estimate=pl.CostEstimate(
            flops=0, bytes_accessed=4 * total * sum(w for _, _, w in cuts), transcendentals=0
        ),
        name="place",
    )(spot, *first, *second)
    return [whole.reshape(total, width) for whole, (_, _, width) in zip(wholes, cuts)]


def pick(values, index, axis):
    return lax.dynamic_index_in_dim(values, index, axis, keepdims=False)


def first_sum(cut, count, send):
    total = cut(0).astype(f32)
    for r in range(1, count):
        total = total + send(cut(r), r).astype(f32)
    return total.astype(bf16)


def send_z(part, r):
    return move_fsdp(part, r, 0, 0)


def send_y(part, r):
    return move_fsdp(part, 0, 0, r)


def scatter_fsdp_one(join, grads, spot):
    z, y = spot[0], spot[2]
    rows = grads[0].shape[0] // FSDP
    views = [g.reshape(NZ, NX, NY, 2, rows // 2, g.shape[1]) for g in grads]
    joined = lambda parts: join([p[None] for p in parts])

    one = first_sum(
        lambda r: joined([pick(v, lax.rem(z + r, NZ), 0)[:, :, 0] for v in views]), NZ, send_z
    )
    two = first_sum(
        lambda r: joined([pick(v, lax.rem(y + r, NY), 2)[:, :, 1] for v in views]), NY, send_y
    )
    return one, two


def scatter_fsdp_two(parts, spot):
    z, x, y = spot[0], spot[1], spot[2]
    one = first_sum(lambda r: pick(parts[0], lax.rem(y + r, NY), 2), NY, send_y)
    two = first_sum(lambda r: pick(parts[1], lax.rem(z + r, NZ), 1), NZ, send_z)
    one, two = lax.optimization_barrier((one, two))

    def last_sum(kept):
        mine, theirs = pick(kept, x, 1), pick(kept, 1 - x, 1)
        return mine.astype(f32) + move_fsdp(theirs, 0, 1, 0).astype(f32)

    return jnp.concatenate([last_sum(one), last_sum(two)], axis=1)


def fill_bias(where, bias):
    size = bias.shape[0]
    rank, end_one, end_two = where[0], where[1], where[2]

    def place_of(index):
        block = lax.div(index, LANES)
        block = 2 * lax.rem(block, 2) + lax.div(block, 2)
        return jnp.bitwise_xor(block, rank) * LANES + lax.rem(index, LANES)

    queries = place_of(lax.broadcasted_iota(jnp.int32, (size, 1), 0))
    keys = place_of(lax.broadcasted_iota(jnp.int32, (1, size), 1))
    start = jnp.where(queries >= end_two, end_two, jnp.where(queries >= end_one, end_one, 0))
    visible = (keys <= queries) & (keys >= start)
    bias[...] = jnp.where(visible, 0.0, -1e30).astype(f32)


def exponents(q_ref, k_ref, bias):
    scores = contract_last(q_ref[...], k_ref[...]) * (HEAD_SIZE**-0.5) + bias[...]
    exponent = jnp.exp(scores - jnp.max(scores, axis=-1, keepdims=True))
    return exponent / jnp.sum(exponent, axis=-1, keepdims=True)


def attend_kernel(where, q_ref, k_ref, v_ref, out_ref, bias):
    @pl.when(pl.program_id(0) == 0)
    def _():
        fill_bias(where, bias)

    probability = exponents(q_ref, k_ref, bias).astype(bf16)
    out_ref[...] = matmul(probability, v_ref[...]).astype(bf16)


def attend(where, qkv, heads):
    rows = qkv.shape[0]
    block = (rows, HEAD_SIZE)
    return pl.pallas_call(
        attend_kernel,
        out_shape=jax.ShapeDtypeStruct((rows, heads * HEAD_SIZE), bf16),
        grid_spec=pltpu.PrefetchScalarGridSpec(
            num_scalar_prefetch=1,
            grid=(heads,),
            in_specs=[
                pl.BlockSpec(block, lambda h, w: (0, h)),
                pl.BlockSpec(block, lambda h, w: (0, heads)),
                pl.BlockSpec(block, lambda h, w: (0, heads + 1)),
            ],
            out_specs=pl.BlockSpec(block, lambda h, w: (0, h)),
            scratch_shapes=[pltpu.VMEM((rows, rows), f32)],
        ),
        compiler_params=pltpu.CompilerParams(vmem_limit_bytes=40 * 1024 * 1024),
        cost_estimate=pl.CostEstimate(
            flops=4 * heads * rows * rows * HEAD_SIZE,
            bytes_accessed=4 * rows * heads * HEAD_SIZE,
            transcendentals=heads * rows * rows,
        ),
        name="attend",
    )(where, qkv, qkv, qkv)


def attend_back_kernel(heads, where, q_ref, k_ref, v_ref, g_ref, out_ref, bias, key_sum, value_sum):
    head = pl.program_id(0)

    @pl.when(head == 0)
    def _():
        fill_bias(where, bias)
        key_sum[...] = jnp.zeros_like(key_sum)
        value_sum[...] = jnp.zeros_like(value_sum)

    scale = HEAD_SIZE**-0.5
    probability = exponents(q_ref, k_ref, bias)
    grad_prob = contract_last(g_ref[...], v_ref[...])
    inner = jnp.sum(probability * grad_prob, axis=-1, keepdims=True)
    grad_scores = (probability * (grad_prob - inner)).astype(bf16)
    columns = pl.ds(pl.multiple_of(head * HEAD_SIZE, HEAD_SIZE), HEAD_SIZE)
    out_ref[:, columns] = (matmul(grad_scores, k_ref[...]) * scale).astype(bf16)
    key_sum[...] += contract_first(grad_scores, q_ref[...])
    value_sum[...] += contract_first(probability.astype(bf16), g_ref[...])

    @pl.when(head == heads - 1)
    def _():
        wide = heads * HEAD_SIZE
        out_ref[:, wide : wide + HEAD_SIZE] = (key_sum[...] * scale).astype(bf16)
        out_ref[:, wide + HEAD_SIZE :] = value_sum[...].astype(bf16)


def attend_back(where, qkv, grads, heads):
    rows = qkv.shape[0]
    block = (rows, HEAD_SIZE)
    return pl.pallas_call(
        functools.partial(attend_back_kernel, heads),
        out_shape=jax.ShapeDtypeStruct(qkv.shape, bf16),
        grid_spec=pltpu.PrefetchScalarGridSpec(
            num_scalar_prefetch=1,
            grid=(heads,),
            in_specs=[
                pl.BlockSpec(block, lambda h, w: (0, h)),
                pl.BlockSpec(block, lambda h, w: (0, heads)),
                pl.BlockSpec(block, lambda h, w: (0, heads + 1)),
                pl.BlockSpec(block, lambda h, w: (0, h)),
            ],
            out_specs=pl.BlockSpec(qkv.shape, lambda h, w: (0, 0)),
            scratch_shapes=[
                pltpu.VMEM((rows, rows), f32),
                pltpu.VMEM(block, f32),
                pltpu.VMEM(block, f32),
            ],
        ),
        compiler_params=pltpu.CompilerParams(vmem_limit_bytes=40 * 1024 * 1024),
        cost_estimate=pl.CostEstimate(
            flops=10 * heads * rows * rows * HEAD_SIZE,
            bytes_accessed=6 * rows * heads * HEAD_SIZE,
            transcendentals=heads * rows * rows,
        ),
        name="attend_back",
    )(where, qkv, qkv, qkv, grads)


def expert_rows_kernel(
    scal, rows_own, gate_lanes, rows_far, grads_own, grads_far,
    eg_own, eg_far, eu_own, eu_far, ed_own, ed_far, d_gate, d_up, hidden, sent_far, dots,
):
    count, width = rows_own.shape[0], eg_own.shape[0]
    experts = dots.shape[1] // 2
    row = lax.broadcasted_iota(jnp.int32, (count, 1), 0) + pl.program_id(0) * count
    second = (lax.rem(row, 2 * CAP) >= CAP).astype(jnp.int32)
    column = (lax.broadcasted_iota(jnp.int32, (1, width), 1) >= width // 2).astype(jnp.int32)
    mine = second == column
    lane = lax.broadcasted_iota(jnp.int32, (1, 2 * experts), 1)
    expert_of = scal[1] + second
    high_lane, low_lane = lane == expert_of, lane == experts + expert_of
    gate_of = jnp.sum(
        jnp.where(high_lane | low_lane, gate_lanes[...].astype(f32), 0.0), axis=1, keepdims=True
    )
    gate_mine = jnp.where(mine, gate_of, 0.0)

    def product(own, far, w_own, w_far):
        return contract_last(own[...], w_own[...]) + contract_last(far[...], w_far[...])

    gate_pre = product(rows_own, rows_far, eg_own, eg_far)
    up_pre = product(rows_own, rows_far, eu_own, eu_far)
    down_back = product(grads_own, grads_far, ed_own, ed_far) * gate_mine
    sigmoid_v = jax.nn.sigmoid(gate_pre)
    silu_gate = gate_pre * sigmoid_v
    hidden_wide = silu_gate * up_pre
    hidden[...] = (hidden_wide * gate_mine).astype(bf16)
    gate_part = (
        down_back * up_pre * (sigmoid_v * (1.0 + gate_pre * (1.0 - sigmoid_v)))
    ).astype(bf16)
    up_part = (down_back * silu_gate).astype(bf16)
    d_gate[...] = gate_part
    d_up[...] = up_part
    sent_far[...] = (matmul(gate_part, eg_far[...]) + matmul(up_part, eu_far[...])).astype(bf16)
    slot_dot = jnp.sum(hidden_wide * down_back, axis=1, keepdims=True)
    high = slot_dot.astype(bf16).astype(f32)
    dots[...] = jnp.where(high_lane, high, jnp.where(low_lane, slot_dot - high, 0.0)).astype(bf16)


def expert_rows(scal, rows_own, rows_far, grads_own, grads_far, gate_w, up_w, down_w, steps=2):
    rows, wide = grads_own.shape
    hidden = gate_w.shape[0]
    count = rows // steps
    block = pl.BlockSpec((count, wide), lambda i, c: (i, 0))
    own = pl.BlockSpec((hidden, wide), lambda i, c: (0, c[0]))
    far = pl.BlockSpec((hidden, wide), lambda i, c: (0, 1 - c[0]))
    narrow = pl.BlockSpec((count, hidden), lambda i, c: (i, 0))
    lanes = pl.BlockSpec((count, LANES), lambda i, c: (i, 0))
    last_lanes = pl.BlockSpec((count, LANES), lambda i, c: (i, wide // LANES))
    shape = lambda columns: jax.ShapeDtypeStruct((rows, columns), bf16)
    return pl.pallas_call(
        expert_rows_kernel,
        out_shape=[shape(hidden), shape(hidden), shape(hidden), shape(wide), shape(LANES)],
        grid_spec=pltpu.PrefetchScalarGridSpec(
            num_scalar_prefetch=1,
            grid=(steps,),
            in_specs=[block, last_lanes] + [block] * 3 + [own, far] * 3,
            out_specs=[narrow] * 3 + [block, lanes],
        ),
        compiler_params=pltpu.CompilerParams(vmem_limit_bytes=56 * 1024 * 1024),
        cost_estimate=pl.CostEstimate(
            flops=16 * rows * wide * hidden,
            bytes_accessed=12 * hidden * wide + 12 * rows * wide,
            transcendentals=rows * hidden,
        ),
        name="expert_rows",
    )(
        scal, rows_own, rows_own, rows_far, grads_own, grads_far,
        gate_w, gate_w, up_w, up_w, down_w, down_w,
    )


def join_kernel(left, right, tail, out):
    wide = left.shape[1]
    out[:, :wide] = (left[...].astype(f32) + right[...].astype(f32)).astype(bf16)
    out[:, wide:] = tail[...]


def add_and_join(left, right, tail, steps=4):
    rows, wide = left.shape
    block = pl.BlockSpec((rows // steps, wide), lambda i: (i, 0))
    return pl.pallas_call(
        join_kernel,
        out_shape=jax.ShapeDtypeStruct((rows, wide + tail.shape[1]), bf16),
        grid=(steps,),
        in_specs=[block, block, pl.BlockSpec((rows // steps, tail.shape[1]), lambda i: (i, 0))],
        out_specs=pl.BlockSpec((rows // steps, wide + tail.shape[1]), lambda i: (i, 0)),
        cost_estimate=pl.CostEstimate(
            flops=rows * wide, bytes_accessed=6 * rows * wide, transcendentals=0
        ),
        name="add_and_join",
    )(left, right, tail)


def combine_kernel(with_logits, core, dispatch, back, base, *refs):
    half = base.shape[1] // 2
    total = matmul(dispatch[...], back[...])
    extra = 0.0
    if with_logits:
        gates, tile, out, logits = refs
        experts = LANES // 2
        lanes = total[:, half:]
        dots = lanes + pltpu.roll(lanes, experts, 1)
        lane = lax.broadcasted_iota(jnp.int32, dots.shape, 1)
        dots = jnp.where(lane < experts, dots, 0.0)
        d_logits = (dots - gates[...] * jnp.sum(dots, axis=-1, keepdims=True)).astype(bf16)
        logits[...] = d_logits
        extra = contract_last(d_logits, tile[...])
    else:
        (out,) = refs
    sums = base[...].astype(f32) + extra
    for number in range(2):
        columns = slice(number * half, (number + 1) * half)
        chosen = jnp.where(core[0] == number, total[:, :half], 0.0)
        out[:, columns] = (sums[:, columns] + chosen).astype(out.dtype)


def combine(core, block, dispatch, back, base, dtype, gates=None, tile=None):
    rows, dim = base.shape[0] // 2, base.shape[1]
    slots, width = back.shape
    with_logits = gates is not None
    part = lambda columns: pl.BlockSpec((rows, columns), lambda i, c: (block, 0))
    whole = lambda shape: pl.BlockSpec(shape, lambda i, c: (0, 0))
    specs = [part(slots), whole((slots, width)), part(dim)]
    args = [dispatch, back, base]
    shapes = [jax.ShapeDtypeStruct((rows, dim), dtype)]
    outs = [whole((rows, dim))]
    if with_logits:
        specs += [part(LANES), whole(tile.shape)]
        args += [gates, tile]
        shapes.append(jax.ShapeDtypeStruct((rows, LANES), bf16))
        outs.append(whole((rows, LANES)))
    return pl.pallas_call(
        functools.partial(combine_kernel, with_logits),
        out_shape=shapes,
        grid_spec=pltpu.PrefetchScalarGridSpec(
            num_scalar_prefetch=1, grid=(1,), in_specs=specs, out_specs=outs
        ),
        compiler_params=pltpu.CompilerParams(vmem_limit_bytes=48 * 1024 * 1024),
        cost_estimate=pl.CostEstimate(
            flops=2 * rows * slots * width,
            bytes_accessed=2 * slots * width + 8 * rows * dim,
            transcendentals=0,
        ),
        name="combine",
    )(core, *args)


def shared_rows_kernel(rows, grads, weights, d_gate, d_up, hidden, out, back):
    def weight(number):
        part = weights[:, number]
        return part.reshape(part.shape[0] * part.shape[1], part.shape[2])

    gate_pre = matmul(rows[...], weight(0))
    up_pre = matmul(rows[...], weight(1))
    down_back = matmul(grads[...], weight(2))
    sigmoid_v = jax.nn.sigmoid(gate_pre)
    silu_gate = gate_pre * sigmoid_v
    hidden_part = (silu_gate * up_pre).astype(bf16)
    hidden[...] = hidden_part
    out[...] = contract_last(hidden_part, weight(2)).astype(bf16)
    gate_part = (
        down_back * up_pre * (sigmoid_v * (1.0 + gate_pre * (1.0 - sigmoid_v)))
    ).astype(bf16)
    up_part = (down_back * silu_gate).astype(bf16)
    d_gate[...] = gate_part
    d_up[...] = up_part
    back[...] = (contract_last(gate_part, weight(0)) + contract_last(up_part, weight(1))).astype(
        bf16
    )


def shared_rows(rows, grads, weights, steps=2):
    count, dim = rows.shape
    hidden = weights.shape[3]
    wide = pl.BlockSpec((count // steps, dim), lambda i: (i, 0))
    narrow = pl.BlockSpec((count // steps, hidden), lambda i: (i, 0))
    shape = lambda columns: jax.ShapeDtypeStruct((count, columns), bf16)
    return pl.pallas_call(
        shared_rows_kernel,
        out_shape=[shape(hidden)] * 3 + [shape(dim)] * 2,
        grid=(steps,),
        in_specs=[wide, wide, pl.BlockSpec(weights.shape, lambda i: (0, 0, 0, 0))],
        out_specs=[narrow] * 3 + [wide] * 2,
        compiler_params=pltpu.CompilerParams(vmem_limit_bytes=56 * 1024 * 1024),
        cost_estimate=pl.CostEstimate(
            flops=12 * count * dim * hidden,
            bytes_accessed=6 * dim * hidden + 8 * count * dim,
            transcendentals=count * hidden,
        ),
        name="shared_rows",
    )(rows, grads, weights)


def shared_grads_kernel(rows, grads, d_gate, d_up, hidden, out):
    number = pl.program_id(0)

    def write(left, right):
        out[...] = contract_first(left[...], right[...]).astype(bf16).reshape(out.shape)

    pl.when(number == 0)(lambda: write(rows, d_gate))
    pl.when(number == 1)(lambda: write(rows, d_up))
    pl.when(number == 2)(lambda: write(grads, hidden))


def shared_grads(rows, grads, d_gate, d_up, hidden, own_rows):
    count, dim = rows.shape
    width = d_gate.shape[1]
    wide = pl.BlockSpec((count, dim), lambda i: (0, 0))
    narrow = pl.BlockSpec((count, width), lambda i: (0, 0))
    return pl.pallas_call(
        shared_grads_kernel,
        out_shape=jax.ShapeDtypeStruct((FSDP, 3, own_rows, width), bf16),
        grid=(3,),
        in_specs=[wide] * 2 + [narrow] * 3,
        out_specs=pl.BlockSpec((FSDP, 1, own_rows, width), lambda i: (0, i, 0, 0)),
        compiler_params=pltpu.CompilerParams(vmem_limit_bytes=48 * 1024 * 1024),
        cost_estimate=pl.CostEstimate(
            flops=6 * count * dim * width,
            bytes_accessed=6 * dim * width + 4 * count * dim,
            transcendentals=0,
        ),
        name="shared_grads",
    )(rows, grads, d_gate, d_up, hidden)


def expert_grads_kernel(core, rows_own, rows_far, grads_own, grads_far, d_gate, d_up, scaled, *outs):
    half = pl.program_id(0)

    def write(rows, grads):
        outs[0][...] = contract_first(d_gate[...], rows[...])
        outs[1][...] = contract_first(d_up[...], rows[...])
        outs[2][...] = contract_first(scaled[...], grads[...])

    pl.when(half == 0)(lambda: write(rows_own, grads_own))
    pl.when(half == 1)(lambda: write(rows_far, grads_far))


def expert_grads(core, rows_own, rows_far, grads_own, grads_far, d_gate, d_up, scaled):
    rows, wide = grads_own.shape
    hidden = d_gate.shape[1]
    full = pl.BlockSpec((rows, wide), lambda h, c: (0, 0))
    part = pl.BlockSpec((rows, hidden), lambda h, c: (0, 0))
    result = pl.BlockSpec((hidden, wide), lambda h, c: (0, jnp.bitwise_xor(h, c[0])))
    return pl.pallas_call(
        expert_grads_kernel,
        out_shape=[jax.ShapeDtypeStruct((hidden, 2 * wide), f32)] * 3,
        grid_spec=pltpu.PrefetchScalarGridSpec(
            num_scalar_prefetch=1,
            grid=(2,),
            in_specs=[full] * 4 + [part] * 3,
            out_specs=[result] * 3,
        ),
        compiler_params=pltpu.CompilerParams(vmem_limit_bytes=56 * 1024 * 1024),
        cost_estimate=pl.CostEstimate(
            flops=12 * rows * wide * hidden,
            bytes_accessed=24 * hidden * wide + 12 * rows * wide,
            transcendentals=0,
        ),
        name="expert_grads",
    )(core, rows_own, rows_far, grads_own, grads_far, d_gate, d_up, scaled)


def per_device(
    tokens,
    g_attn,
    query_matrix,
    key_matrix,
    value_matrix,
    w_out,
    g_ffn,
    w_router,
    shared_gate,
    shared_up,
    shared_down,
    expert_gate,
    expert_up,
    expert_down,
    lengths,
    routes,
    cotangent,
):
    tok_dev, dim = tokens.shape
    group_rows = tok_dev * TP
    near = group_rows // 2
    experts = w_router.shape[1]
    own_rows = w_router.shape[0]
    q_width, kv_width = query_matrix.shape[1], key_matrix.shape[1]
    qkv_width = q_width + 2 * kv_width
    heads = q_width // HEAD_SIZE
    local_experts, _, hidden_own = expert_gate.shape
    half_dim = dim // 2
    fsdp_at = lax.axis_index("fsdp")
    rank = lax.axis_index("tp")
    core = lax.rem(rank, 2)
    core_vec = core.astype(jnp.int32).reshape(1)
    spot = jnp.stack(
        [fsdp_at // (NX * NY), lax.rem(fsdp_at // NY, NX), lax.rem(fsdp_at, NY)]
    ).astype(jnp.int32)

    route_blocks = routes.reshape(TP, tok_dev, routes.shape[1])
    own_routes = jnp.concatenate(
        [pick(route_blocks, jnp.bitwise_xor(b, rank), 0) for b in BLOCK_ORDER], axis=0
    )
    places = jnp.concatenate(
        [jnp.bitwise_xor(b, rank) * tok_dev + jnp.arange(tok_dev) for b in BLOCK_ORDER]
    ).astype(jnp.int32)
    expert_lane = jnp.arange(LANES, dtype=jnp.int32)[None, :]
    hot = (own_routes[:, 0:1] == expert_lane) | (own_routes[:, 1:2] == expert_lane)
    before = (places[None, :] < places[:, None]).astype(bf16)
    earlier = matmul(before, hot.astype(bf16))
    slots = experts * CAP
    slot_ids = jnp.arange(slots, dtype=jnp.int32)
    spread = (slot_ids[None, :] // CAP == jnp.arange(LANES, dtype=jnp.int32)[:, None]).astype(bf16)
    slot_wanted = matmul(jnp.where(hot, earlier, -1.0).astype(bf16), spread)
    dispatch = (slot_wanted == (slot_ids % CAP).astype(f32)[None, :]).astype(bf16)

    def core_half(values):
        return lax.dynamic_slice_in_dim(values, core * half_dim, half_dim, 1)

    small_tile = jnp.concatenate(
        [
            w_router,
            g_attn[:, None],
            g_ffn[:, None],
            jnp.zeros((own_rows, LANES - experts - 2), bf16),
        ],
        axis=1,
    )
    qkv_own = jnp.concatenate([query_matrix, key_matrix, value_matrix], axis=1)
    lines = gather_lines(
        gather_pair(jnp.concatenate([qkv_own, small_tile, w_out], axis=1)[None])
    )
    near_lines = gather_near(lines)
    token_pair = jnp.concatenate([tokens, after(move_tp(tokens, 2), *near_lines)], axis=0)
    token_rows = jnp.concatenate([token_pair, move_tp(token_pair, 1)], axis=0)
    grad_pair = jnp.concatenate([cotangent, after(move_tp(cotangent, 2), *near_lines)], axis=0)
    grad_rows = jnp.concatenate([grad_pair, move_tp(grad_pair, 1)], axis=0)
    w_qkv, w_tile, w_out_all = gather_all(
        lines,
        near_lines,
        spot,
        (
            (0, 0, qkv_width),
            (0, qkv_width, LANES),
            (0, qkv_width + LANES, q_width),
        ),
    )
    slot_grads = contract_first(dispatch, core_half(grad_rows)).astype(bf16)
    grads_own = swap_fsdp(after(slot_grads, w_tile))
    shared_own = jnp.concatenate([shared_gate, shared_up, shared_down], axis=0)
    w_shared = lax.all_gather(
        after(shared_own, w_tile), "fsdp", axis=0, tiled=True
    ).reshape(FSDP, 3, own_rows, shared_gate.shape[1])
    lane = lax.broadcasted_iota(jnp.int32, (8, LANES), 1)
    gain_pick = (lane == experts + lax.broadcasted_iota(jnp.int32, (8, LANES), 0)).astype(bf16)
    gains = contract_last(gain_pick, w_tile)
    gain_one, gain_two = gains[0:1], gains[1:2]

    hidden_all = local_experts * hidden_own

    def by_hidden(weights):
        return jnp.swapaxes(weights, 1, 2).reshape(hidden_all, dim)

    gate_w, up_w, down_w = by_hidden(expert_gate), by_hidden(expert_up), by_hidden(expert_down)

    ends = jnp.cumsum(lengths[0])
    where = jnp.stack([rank.astype(jnp.int32), ends[0], ends[1]]).astype(jnp.int32)
    normed_one, _ = norm_rows(token_rows.astype(f32), gain_one)
    h_attn = normed_one.astype(bf16)
    qkv = matmul(h_attn, w_qkv).astype(bf16)
    attended = attend(where, qkv, heads)
    attn_far = after(contract_last(attended[near:], w_out_all).astype(bf16), grads_own)
    attn_own = scatter_tp(contract_last(attended[:near], w_out_all), attn_far)
    own_tokens = tokens.astype(f32)
    middle = own_tokens + attn_own
    normed_two, factor_two = norm_rows(middle, gain_two)
    h_ffn = gather_tp(normed_two.astype(bf16))

    logits = matmul(h_ffn, w_tile)
    top = jnp.max(jnp.where(hot, logits, -1e30), axis=-1, keepdims=True)
    gate_exp = jnp.where(hot, jnp.exp(jnp.minimum(logits - top, 0.0)), 0.0)
    gates = gate_exp / jnp.sum(gate_exp, axis=-1, keepdims=True)
    gate_high = gates.astype(bf16)
    gate_low = (gates - gate_high.astype(f32)).astype(bf16)
    gate_lanes = jnp.concatenate([gate_high[:, :experts], gate_low[:, :experts]], axis=1)

    slot_rows = contract_first(
        dispatch, jnp.concatenate([core_half(h_ffn), gate_lanes], axis=1)
    ).astype(bf16)
    grads_far = move_tp(after(grads_own, slot_rows), 1)
    rows_own = swap_fsdp(slot_rows)

    rows_far = move_tp(rows_own, 1)
    scal = jnp.stack([core.astype(jnp.int32), local_experts * fsdp_at.astype(jnp.int32)])
    d_gate, d_up, hidden, sent_far, dot_lanes = expert_rows(
        scal, rows_own, rows_far, grads_own, grads_far, gate_w, up_w, down_w
    )
    sent_far = move_tp(sent_far, 1)
    sent_own = (matmul(d_gate, core_half(gate_w)) + matmul(d_up, core_half(up_w))).astype(bf16)
    payload = add_and_join(sent_own, sent_far, dot_lanes)
    returned = swap_fsdp(payload)

    h_then = after(h_ffn, payload)
    s_d_gate, s_d_up, s_hidden, shared_out, shared_back = shared_rows(h_then, grad_rows, w_shared)
    shared_parts = shared_grads(h_then, grad_rows, s_d_gate, s_d_up, s_hidden, own_rows)
    shared_sums = staged_sum(shared_parts)[0].astype(f32)

    hidden_then = after(hidden, payload)
    down_own = core_half(down_w)
    down_far = lax.dynamic_slice_in_dim(down_w, (1 - core) * half_dim, half_dim, 1)
    out_far = move_tp(matmul(hidden_then, down_far).astype(bf16), 1)
    out_own = (matmul(hidden_then, down_own) + out_far.astype(f32)).astype(bf16)

    def expert_layout(grads):
        return jnp.swapaxes(grads.reshape(local_experts, hidden_own, dim), 1, 2)

    returned = after(returned, shared_back, shared_parts, out_own)
    ffn_far, logits_far = combine(
        core_vec, 1, dispatch, returned, shared_back, bf16, gates, w_tile
    )
    ffn_near, logits_near = combine(
        core_vec, 0, dispatch, returned, shared_back, f32, gates, w_tile
    )
    d_h_ffn = scatter_tp(ffn_near, ffn_far)
    d_middle = cotangent.astype(f32) + norm_back(middle, factor_two, gain_two, d_h_ffn)
    lane_ids = lax.broadcasted_iota(jnp.int32, (1, LANES), 1)
    gain_terms = (d_h_ffn * middle * factor_two).astype(bf16)
    gain_lane = jnp.broadcast_to(lane_ids == experts, (tok_dev, LANES)).astype(bf16)
    d_att_own = d_middle.astype(bf16)
    d_att_near = jnp.concatenate([d_att_own, move_tp(d_att_own, 2)], axis=0)
    out_back = swap_fsdp(after(out_own, d_att_near))
    d_att = jnp.concatenate([d_att_near, move_tp(d_att_near, 1)], axis=0)
    grad_tile = (
        contract_first(h_ffn, jnp.concatenate([logits_near, logits_far], axis=0))
        + contract_first(gain_terms, gain_lane)
    ).astype(bf16)
    grad_wout = contract_first(d_att, attended).astype(bf16)
    d_attended = matmul(d_att, w_out_all).astype(bf16)
    d_qkv = attend_back(where, qkv, d_attended, heads)
    grad_wqkv = contract_first(h_attn, d_qkv).astype(bf16)
    sum_parts = scatter_fsdp_one(
        lambda parts: jnp.concatenate(parts, axis=-1), [grad_wout, grad_tile, grad_wqkv], spot
    )
    attn_far = contract_last(d_qkv[near:], w_qkv).astype(bf16)
    d_h_attn = scatter_tp(contract_last(d_qkv[:near], w_qkv), attn_far)
    back_then = after(out_back, attn_far)
    (out_far,) = combine(core_vec, 1, dispatch, back_then, shared_out, bf16)
    (out_near,) = combine(core_vec, 0, dispatch, back_then, shared_out, f32)
    output = (middle + scatter_tp(out_near, out_far)).astype(bf16)
    grad_egate, grad_eup, grad_edown = expert_grads(
        core_vec, rows_own, rows_far, grads_own, grads_far, d_gate, d_up, after(hidden, grad_wqkv)
    )
    sum_parts = after(sum_parts, d_h_attn, out_near, grad_egate)
    sums = scatter_fsdp_two(sum_parts, spot)[0]
    out_sums, tile_sums = sums[:, :q_width], small_sum_tp(sums[:, q_width : q_width + LANES])
    qkv_sums = sums[:, q_width + LANES :]
    _, factor_one = norm_rows(own_tokens, gain_one)
    grad_tokens = (d_middle + norm_back(own_tokens, factor_one, gain_one, d_h_attn)).astype(bf16)
    gain_sum = jnp.sum(qkv_sums * qkv_own.astype(f32), axis=1)
    grad_g_attn = small_sum_tp(gain_sum) / g_attn.astype(f32)
    return (
        output,
        grad_tokens,
        grad_g_attn,
        qkv_sums[:, :q_width],
        qkv_sums[:, q_width : q_width + kv_width],
        qkv_sums[:, q_width + kv_width :],
        out_sums,
        tile_sums[:, experts],
        tile_sums[:, :experts],
        shared_sums[0],
        shared_sums[1],
        shared_sums[2],
        expert_layout(grad_egate),
        expert_layout(grad_eup),
        expert_layout(grad_edown),
    )


def solution(mesh):
    in_specs = (
        P(("fsdp", "tp"), None),
        P("fsdp"),
        P("fsdp", "tp"),
        P("fsdp", "tp"),
        P("fsdp", "tp"),
        P("fsdp", "tp"),
        P("fsdp"),
        P("fsdp", None),
        P("fsdp", "tp"),
        P("fsdp", "tp"),
        P("fsdp", "tp"),
        P("fsdp", None, "tp"),
        P("fsdp", None, "tp"),
        P("fsdp", None, "tp"),
        P("fsdp", None),
        P("fsdp", None),
        P(("fsdp", "tp"), None),
    )
    out_specs = (
        P(("fsdp", "tp"), None),
        P(("fsdp", "tp"), None),
        P("fsdp"),
        P("fsdp", "tp"),
        P("fsdp", "tp"),
        P("fsdp", "tp"),
        P("fsdp", "tp"),
        P("fsdp"),
        P("fsdp", None),
        P("fsdp", "tp"),
        P("fsdp", "tp"),
        P("fsdp", "tp"),
        P("fsdp", None, "tp"),
        P("fsdp", None, "tp"),
        P("fsdp", None, "tp"),
    )
    return jax.shard_map(
        per_device, mesh=mesh, in_specs=in_specs, out_specs=out_specs, check_vma=False
    )
```

```python
import functools

import jax
import jax.numpy as jnp
from jax import lax
from jax.experimental import pallas as pl
from jax.experimental.pallas import tpu as pltpu
from jax.sharding import PartitionSpec as P

HEAD_SIZE = 128
NZ, NX, NY = 4, 2, 4
FSDP = NZ * NX * NY
TP = 4
CAP = 20
LANES = 128
BLOCK_ORDER = (0, 2, 1, 3)
bf16 = jnp.bfloat16
f32 = jnp.float32

epsilon = 1e-06


def contract_first(left_op, right_op):
    return lax.dot_general(
        left_op, right_op, (((0,), (0,)), ((), ())), preferred_element_type=f32
    )


def contract_last(left_op, right_op):
    return lax.dot_general(
        left_op, right_op, (((1,), (1,)), ((), ())), preferred_element_type=f32
    )


def matmul(left_op, right_op):
    return jnp.dot(left_op, right_op, preferred_element_type=f32)


def silu_slope(values):
    sigmoid_v = jax.nn.sigmoid(values)
    return sigmoid_v * (1.0 + values * (1.0 - sigmoid_v))


def norm_rows(values, gain_vec):
    factor = lax.rsqrt(jnp.mean(values * values, axis=-1, keepdims=True) + epsilon)
    return (values * factor * gain_vec, factor)


def norm_back(values, factor, gain_vec, upstream):
    scaled_up = upstream * gain_vec
    return factor * scaled_up - values * factor * factor * factor * jnp.mean(
        scaled_up * values, axis=-1, keepdims=True
    )


def after(value, *earlier):
    return lax.optimization_barrier((value, *earlier))[0]


def swap_along(values, fz, fx, fy):
    return route_fsdp(values, lambda z, x, y: (z ^ fz, x ^ fx, y ^ fy))


def route_fsdp(values, target):
    pairs = []
    for z in range(NZ):
        for x in range(NX):
            for y in range(NY):
                to_z, to_x, to_y = target(z, x, y)
                pairs.append(((z * NX + x) * NY + y, (to_z * NX + to_x) * NY + to_y))
    return lax.ppermute(values, "fsdp", pairs)


def move_tp(values, flip):
    return lax.ppermute(values, "tp", [(i, i ^ flip) for i in range(TP)])


def gather_tp(own):
    pair = jnp.concatenate([own, move_tp(own, 2)], axis=0)
    return jnp.concatenate([pair, move_tp(pair, 1)], axis=0)


def sum_cores(near_part, far_part):
    return near_part + move_tp(far_part.astype(bf16), 1).astype(f32)


def sum_chips(summed):
    rows = summed.shape[0] // 2
    return summed[:rows] + move_tp(summed[rows:].astype(bf16), 2).astype(f32)


def small_sum_tp(values):
    return values + move_tp(values, 1) + move_tp(values, 2) + move_tp(values, 3)


def swap_fsdp(values):
    shape = values.shape
    blocks = values.reshape(FSDP, shape[0] // FSDP, shape[1])
    return lax.all_to_all(blocks, "fsdp", split_axis=0, concat_axis=0, tiled=True).reshape(shape)


def sum_along_z(values):
    lines = [[z * NX * NY + i for z in range(NZ)] for i in range(NX * NY)]
    return lax.psum_scatter(
        values, "fsdp", scatter_dimension=0, tiled=True, axis_index_groups=lines
    )


def sum_across(values):
    planes = [[z * NX * NY + i for i in range(NX * NY)] for z in range(NZ)]
    parts = lax.all_to_all(
        values, "fsdp", split_axis=0, concat_axis=0, tiled=True, axis_index_groups=planes
    )
    return jnp.sum(parts.astype(f32), axis=0)


def place_kernel(cuts, spot, *refs):
    pieces, outs, held, sems = refs[:10], refs[10 : 10 + len(cuts)], refs[-11:-1], refs[-1]
    z, x, y = spot[0], spot[1], spot[2]
    half = pieces[0].shape[3]
    copies = [pltpu.make_async_copy(pieces[i], held[i], sems.at[i]) for i in range(10)]
    for copy in copies:
        copy.start()
    for number in range(10):
        copies[number].wait()
        lines, across = divmod(number, 5)
        opposite = across in (2, 3)
        for place in range(held[number].shape[0]):
            along_line = place + 2 * (across == 3)
            step = 2 if opposite else (0, 1, 2, 2, 3)[across]
            zr, yr = (step, along_line) if lines == 0 else (along_line, step)
            rows = slice(lines * half, (lines + 1) * half)
            for xr in range(NX):
                at = (jnp.bitwise_xor(z, zr), jnp.bitwise_xor(x, xr), jnp.bitwise_xor(y, yr))
                for out, (item, start, width) in zip(outs, cuts):
                    out[at[0], at[1], at[2], rows] = held[number][
                        place, xr, item, :, start : start + width
                    ]


def gather_pair(stacked):
    half = stacked.shape[1] // 2
    pair = jnp.stack([stacked, swap_along(stacked, 0, 1, 0)])
    return pair[:, :, :half], pair[:, :, half:]


def gather_lines(pair):
    near_y, near_z = pair
    by_y = jnp.stack([near_y] + [swap_along(near_y, 0, 0, r) for r in range(1, NY)])
    by_z = jnp.stack([near_z] + [swap_along(near_z, r, 0, 0) for r in range(1, NZ)])
    return lax.optimization_barrier((by_y, by_z))


def gather_near(lines):
    by_y, by_z = lines
    return lax.optimization_barrier(
        (
            swap_along(by_y, 1, 0, 0),
            swap_along(by_y, 3, 0, 0),
            swap_along(by_z, 0, 0, 1),
            swap_along(by_z, 0, 0, 3),
        )
    )


def gather_all(lines, near, spot, cuts):
    by_y, by_z = lines
    rows = 2 * by_y.shape[3]
    first = [by_y, near[0], swap_along(near[0][:2], 3, 0, 0), swap_along(near[1][2:], 1, 0, 0), near[1]]
    second = [by_z, near[2], swap_along(near[2][:2], 0, 0, 3), swap_along(near[3][2:], 0, 0, 1), near[3]]
    total = FSDP * rows
    wholes = pl.pallas_call(
        functools.partial(place_kernel, cuts),
        out_shape=[jax.ShapeDtypeStruct((NZ, NX, NY, rows, width), bf16) for _, _, width in cuts],
        in_specs=[pl.BlockSpec(memory_space=pltpu.SMEM)]
        + [pl.BlockSpec(memory_space=pl.ANY)] * 10,
        out_specs=[pl.BlockSpec(memory_space=pltpu.VMEM)] * len(cuts),
        scratch_shapes=[pltpu.VMEM(piece.shape, bf16) for piece in first + second]
        + [pltpu.SemaphoreType.DMA((10,))],
        compiler_params=pltpu.CompilerParams(vmem_limit_bytes=60 * 1024 * 1024),
        cost_estimate=pl.CostEstimate(
            flops=0, bytes_accessed=4 * total * sum(w for _, _, w in cuts), transcendentals=0
        ),
        name="place",
    )(spot, *first, *second)
    return [whole.reshape(total, width) for whole, (_, _, width) in zip(wholes, cuts)]


def pick(values, index, axis):
    return lax.dynamic_index_in_dim(values, index, axis, keepdims=False)


def add_up(own, received):
    total = own.astype(f32)
    for part in received:
        total = total + part.astype(f32)
    return total.astype(bf16)


def trade_pieces(pieces):
    for_z, for_y = pieces
    near = [swap_along(for_z[1], 1, 0, 0), swap_along(for_z[3], 3, 0, 0)]
    across = [swap_along(for_y[1], 0, 0, 1), swap_along(for_y[3], 0, 0, 3)]
    near.append(swap_along(for_z[2], 2, 0, 0))
    across.append(swap_along(for_y[2], 0, 0, 2))
    return near, across


def add_pieces(own_z, own_y, received):
    return lax.optimization_barrier((add_up(own_z, received[0]), add_up(own_y, received[1])))


def write_pieces(spot, whole, item, for_z, for_y):
    for r in range(NZ):
        for_z[r][item] = whole[jnp.bitwise_xor(spot[0], r), :, :, 0]
    for r in range(NY):
        for_y[r][item] = whole[:, :, jnp.bitwise_xor(spot[2], r), 1]


def piece_shapes(items, half, columns):
    return [jax.ShapeDtypeStruct((items, NX, NY, half, columns), bf16)] * NZ + [
        jax.ShapeDtypeStruct((items, NZ, NX, half, columns), bf16)
    ] * NY


def scatter_fsdp_two(parts, spot):
    z, x, y = spot[0], spot[1], spot[2]
    halves = (
        [pick(parts[0], jnp.bitwise_xor(y, r), 2) for r in range(NY)],
        [pick(parts[1], jnp.bitwise_xor(z, r), 1) for r in range(NZ)],
    )
    in_z, in_y = trade_pieces((halves[1], halves[0]))
    one, two = lax.optimization_barrier((add_up(halves[0][0], in_y), add_up(halves[1][0], in_z)))

    def last_sum(kept):
        mine, theirs = pick(kept, x, 1), pick(kept, 1 - x, 1)
        return mine.astype(f32) + swap_along(theirs, 0, 1, 0).astype(f32)

    return jnp.concatenate([last_sum(one), last_sum(two)], axis=1)


def fill_bias(where, bias):
    size = bias.shape[0]
    rank, end_one, end_two = where[0], where[1], where[2]

    def place_of(index):
        block = lax.div(index, LANES)
        block = 2 * lax.rem(block, 2) + lax.div(block, 2)
        return jnp.bitwise_xor(block, rank) * LANES + lax.rem(index, LANES)

    queries = place_of(lax.broadcasted_iota(jnp.int32, (size, 1), 0))
    keys = place_of(lax.broadcasted_iota(jnp.int32, (1, size), 1))
    start = jnp.where(queries >= end_two, end_two, jnp.where(queries >= end_one, end_one, 0))
    visible = (keys <= queries) & (keys >= start)
    bias[...] = jnp.where(visible, 0.0, -1e30).astype(f32)


def exponents(q_ref, k_ref, bias):
    scores = contract_last(q_ref[...], k_ref[...]) * (HEAD_SIZE**-0.5) + bias[...]
    exponent = jnp.exp(scores - jnp.max(scores, axis=-1, keepdims=True))
    return exponent / jnp.sum(exponent, axis=-1, keepdims=True)


def attend_kernel(where, q_ref, k_ref, v_ref, out_ref, bias):
    @pl.when(pl.program_id(0) == 0)
    def _():
        fill_bias(where, bias)

    probability = exponents(q_ref, k_ref, bias).astype(bf16)
    out_ref[...] = matmul(probability, v_ref[...]).astype(bf16)


def attend(where, qkv, heads):
    rows = qkv.shape[0]
    block = (rows, HEAD_SIZE)
    return pl.pallas_call(
        attend_kernel,
        out_shape=jax.ShapeDtypeStruct((rows, heads * HEAD_SIZE), bf16),
        grid_spec=pltpu.PrefetchScalarGridSpec(
            num_scalar_prefetch=1,
            grid=(heads,),
            in_specs=[
                pl.BlockSpec(block, lambda h, w: (0, h)),
                pl.BlockSpec(block, lambda h, w: (0, heads)),
                pl.BlockSpec(block, lambda h, w: (0, heads + 1)),
            ],
            out_specs=pl.BlockSpec(block, lambda h, w: (0, h)),
            scratch_shapes=[pltpu.VMEM((rows, rows), f32)],
        ),
        compiler_params=pltpu.CompilerParams(vmem_limit_bytes=40 * 1024 * 1024),
        cost_estimate=pl.CostEstimate(
            flops=4 * heads * rows * rows * HEAD_SIZE,
            bytes_accessed=4 * rows * heads * HEAD_SIZE,
            transcendentals=heads * rows * rows,
        ),
        name="attend",
    )(where, qkv, qkv, qkv)


def attend_back_kernel(heads, where, q_ref, k_ref, v_ref, g_ref, out_ref, bias, key_sum, value_sum):
    head = pl.program_id(0)

    @pl.when(head == 0)
    def _():
        fill_bias(where, bias)
        key_sum[...] = jnp.zeros_like(key_sum)
        value_sum[...] = jnp.zeros_like(value_sum)

    scale = HEAD_SIZE**-0.5
    probability = exponents(q_ref, k_ref, bias)
    grad_prob = contract_last(g_ref[...], v_ref[...])
    inner = jnp.sum(probability * grad_prob, axis=-1, keepdims=True)
    grad_scores = (probability * (grad_prob - inner)).astype(bf16)
    columns = pl.ds(pl.multiple_of(head * HEAD_SIZE, HEAD_SIZE), HEAD_SIZE)
    out_ref[:, columns] = (matmul(grad_scores, k_ref[...]) * scale).astype(bf16)
    key_sum[...] += contract_first(grad_scores, q_ref[...])
    value_sum[...] += contract_first(probability.astype(bf16), g_ref[...])

    @pl.when(head == heads - 1)
    def _():
        wide = heads * HEAD_SIZE
        out_ref[:, wide : wide + HEAD_SIZE] = (key_sum[...] * scale).astype(bf16)
        out_ref[:, wide + HEAD_SIZE :] = value_sum[...].astype(bf16)


def attend_back(where, qkv, grads, heads):
    rows = qkv.shape[0]
    block = (rows, HEAD_SIZE)
    return pl.pallas_call(
        functools.partial(attend_back_kernel, heads),
        out_shape=jax.ShapeDtypeStruct(qkv.shape, bf16),
        grid_spec=pltpu.PrefetchScalarGridSpec(
            num_scalar_prefetch=1,
            grid=(heads,),
            in_specs=[
                pl.BlockSpec(block, lambda h, w: (0, h)),
                pl.BlockSpec(block, lambda h, w: (0, heads)),
                pl.BlockSpec(block, lambda h, w: (0, heads + 1)),
                pl.BlockSpec(block, lambda h, w: (0, h)),
            ],
            out_specs=pl.BlockSpec(qkv.shape, lambda h, w: (0, 0)),
            scratch_shapes=[
                pltpu.VMEM((rows, rows), f32),
                pltpu.VMEM(block, f32),
                pltpu.VMEM(block, f32),
            ],
        ),
        compiler_params=pltpu.CompilerParams(vmem_limit_bytes=40 * 1024 * 1024),
        cost_estimate=pl.CostEstimate(
            flops=10 * heads * rows * rows * HEAD_SIZE,
            bytes_accessed=6 * rows * heads * HEAD_SIZE,
            transcendentals=heads * rows * rows,
        ),
        name="attend_back",
    )(where, qkv, qkv, qkv, grads)


def expert_rows_kernel(
    scal, rows_own, gate_lanes, rows_far, grads_own, grads_far,
    eg_own, eg_far, eu_own, eu_far, ed_own, ed_far, d_gate, d_up, hidden, sent_far, dots,
):
    count, width = rows_own.shape[0], eg_own.shape[0]
    experts = dots.shape[1] // 2
    row = lax.broadcasted_iota(jnp.int32, (count, 1), 0) + pl.program_id(0) * count
    second = (lax.rem(row, 2 * CAP) >= CAP).astype(jnp.int32)
    column = (lax.broadcasted_iota(jnp.int32, (1, width), 1) >= width // 2).astype(jnp.int32)
    mine = second == column
    lane = lax.broadcasted_iota(jnp.int32, (1, 2 * experts), 1)
    expert_of = scal[1] + second
    high_lane, low_lane = lane == expert_of, lane == experts + expert_of
    gate_of = jnp.sum(
        jnp.where(high_lane | low_lane, gate_lanes[...].astype(f32), 0.0), axis=1, keepdims=True
    )
    gate_mine = jnp.where(mine, gate_of, 0.0)

    def product(own, far, w_own, w_far):
        return contract_last(own[...], w_own[...]) + contract_last(far[...], w_far[...])

    gate_pre = product(rows_own, rows_far, eg_own, eg_far)
    up_pre = product(rows_own, rows_far, eu_own, eu_far)
    down_back = product(grads_own, grads_far, ed_own, ed_far) * gate_mine
    sigmoid_v = jax.nn.sigmoid(gate_pre)
    silu_gate = gate_pre * sigmoid_v
    hidden_wide = silu_gate * up_pre
    hidden[...] = (hidden_wide * gate_mine).astype(bf16)
    gate_part = (
        down_back * up_pre * (sigmoid_v * (1.0 + gate_pre * (1.0 - sigmoid_v)))
    ).astype(bf16)
    up_part = (down_back * silu_gate).astype(bf16)
    d_gate[...] = gate_part
    d_up[...] = up_part
    sent_far[...] = (matmul(gate_part, eg_far[...]) + matmul(up_part, eu_far[...])).astype(bf16)
    slot_dot = jnp.sum(hidden_wide * down_back, axis=1, keepdims=True)
    high = slot_dot.astype(bf16).astype(f32)
    dots[...] = jnp.where(high_lane, high, jnp.where(low_lane, slot_dot - high, 0.0)).astype(bf16)


def expert_rows(scal, rows_own, rows_far, grads_own, grads_far, gate_w, up_w, down_w, steps=2):
    rows, wide = grads_own.shape
    hidden = gate_w.shape[0]
    count = rows // steps
    block = pl.BlockSpec((count, wide), lambda i, c: (i, 0))
    own = pl.BlockSpec((hidden, wide), lambda i, c: (0, c[0]))
    far = pl.BlockSpec((hidden, wide), lambda i, c: (0, 1 - c[0]))
    narrow = pl.BlockSpec((count, hidden), lambda i, c: (i, 0))
    lanes = pl.BlockSpec((count, LANES), lambda i, c: (i, 0))
    last_lanes = pl.BlockSpec((count, LANES), lambda i, c: (i, wide // LANES))
    shape = lambda columns: jax.ShapeDtypeStruct((rows, columns), bf16)
    return pl.pallas_call(
        expert_rows_kernel,
        out_shape=[shape(hidden), shape(hidden), shape(hidden), shape(wide), shape(LANES)],
        grid_spec=pltpu.PrefetchScalarGridSpec(
            num_scalar_prefetch=1,
            grid=(steps,),
            in_specs=[block, last_lanes] + [block] * 3 + [own, far] * 3,
            out_specs=[narrow] * 3 + [block, lanes],
        ),
        compiler_params=pltpu.CompilerParams(vmem_limit_bytes=56 * 1024 * 1024),
        cost_estimate=pl.CostEstimate(
            flops=16 * rows * wide * hidden,
            bytes_accessed=12 * hidden * wide + 12 * rows * wide,
            transcendentals=rows * hidden,
        ),
        name="expert_rows",
    )(
        scal, rows_own, rows_own, rows_far, grads_own, grads_far,
        gate_w, gate_w, up_w, up_w, down_w, down_w,
    )


def join_kernel(left, right, tail, out):
    wide = left.shape[1]
    out[:, :wide] = (left[...].astype(f32) + right[...].astype(f32)).astype(bf16)
    out[:, wide:] = tail[...]


def add_and_join(left, right, tail, steps=4):
    rows, wide = left.shape
    block = pl.BlockSpec((rows // steps, wide), lambda i: (i, 0))
    return pl.pallas_call(
        join_kernel,
        out_shape=jax.ShapeDtypeStruct((rows, wide + tail.shape[1]), bf16),
        grid=(steps,),
        in_specs=[block, block, pl.BlockSpec((rows // steps, tail.shape[1]), lambda i: (i, 0))],
        out_specs=pl.BlockSpec((rows // steps, wide + tail.shape[1]), lambda i: (i, 0)),
        cost_estimate=pl.CostEstimate(
            flops=rows * wide, bytes_accessed=6 * rows * wide, transcendentals=0
        ),
        name="add_and_join",
    )(left, right, tail)


def combine_kernel(with_logits, core, dispatch, back, base, *refs):
    half = base.shape[1] // 2
    total = matmul(dispatch[...], back[...])
    extra = 0.0
    if with_logits:
        gates, tile, out, logits = refs
        experts = LANES // 2
        lanes = total[:, half:]
        dots = lanes + pltpu.roll(lanes, experts, 1)
        lane = lax.broadcasted_iota(jnp.int32, dots.shape, 1)
        dots = jnp.where(lane < experts, dots, 0.0)
        d_logits = (dots - gates[...] * jnp.sum(dots, axis=-1, keepdims=True)).astype(bf16)
        logits[...] = d_logits
        extra = contract_last(d_logits, tile[...])
    else:
        (out,) = refs
    sums = base[...].astype(f32) + extra
    for number in range(2):
        columns = slice(number * half, (number + 1) * half)
        chosen = jnp.where(core[0] == number, total[:, :half], 0.0)
        out[:, columns] = (sums[:, columns] + chosen).astype(out.dtype)


def combine(core, block, dispatch, back, base, dtype, gates=None, tile=None):
    rows, dim = base.shape[0] // 2, base.shape[1]
    slots, width = back.shape
    with_logits = gates is not None
    part = lambda columns: pl.BlockSpec((rows, columns), lambda i, c: (block, 0))
    whole = lambda shape: pl.BlockSpec(shape, lambda i, c: (0, 0))
    specs = [part(slots), whole((slots, width)), part(dim)]
    args = [dispatch, back, base]
    shapes = [jax.ShapeDtypeStruct((rows, dim), dtype)]
    outs = [whole((rows, dim))]
    if with_logits:
        specs += [part(LANES), whole(tile.shape)]
        args += [gates, tile]
        shapes.append(jax.ShapeDtypeStruct((rows, LANES), bf16))
        outs.append(whole((rows, LANES)))
    return pl.pallas_call(
        functools.partial(combine_kernel, with_logits),
        out_shape=shapes,
        grid_spec=pltpu.PrefetchScalarGridSpec(
            num_scalar_prefetch=1, grid=(1,), in_specs=specs, out_specs=outs
        ),
        compiler_params=pltpu.CompilerParams(vmem_limit_bytes=48 * 1024 * 1024),
        cost_estimate=pl.CostEstimate(
            flops=2 * rows * slots * width,
            bytes_accessed=2 * slots * width + 8 * rows * dim,
            transcendentals=0,
        ),
        name="combine",
    )(core, *args)


def shared_rows_kernel(rows, grads, weights, d_gate, d_up, hidden, out, back):
    def weight(number):
        part = weights[:, number]
        return part.reshape(part.shape[0] * part.shape[1], part.shape[2])

    gate_pre = matmul(rows[...], weight(0))
    up_pre = matmul(rows[...], weight(1))
    down_back = matmul(grads[...], weight(2))
    sigmoid_v = jax.nn.sigmoid(gate_pre)
    silu_gate = gate_pre * sigmoid_v
    hidden_part = (silu_gate * up_pre).astype(bf16)
    hidden[...] = hidden_part
    out[...] = contract_last(hidden_part, weight(2)).astype(bf16)
    gate_part = (
        down_back * up_pre * (sigmoid_v * (1.0 + gate_pre * (1.0 - sigmoid_v)))
    ).astype(bf16)
    up_part = (down_back * silu_gate).astype(bf16)
    d_gate[...] = gate_part
    d_up[...] = up_part
    back[...] = (contract_last(gate_part, weight(0)) + contract_last(up_part, weight(1))).astype(
        bf16
    )


def shared_rows(rows, grads, weights, steps=2):
    count, dim = rows.shape
    hidden = weights.shape[3]
    wide = pl.BlockSpec((count // steps, dim), lambda i: (i, 0))
    narrow = pl.BlockSpec((count // steps, hidden), lambda i: (i, 0))
    shape = lambda columns: jax.ShapeDtypeStruct((count, columns), bf16)
    return pl.pallas_call(
        shared_rows_kernel,
        out_shape=[shape(hidden)] * 3 + [shape(dim)] * 2,
        grid=(steps,),
        in_specs=[wide, wide, pl.BlockSpec(weights.shape, lambda i: (0, 0, 0, 0))],
        out_specs=[narrow] * 3 + [wide] * 2,
        compiler_params=pltpu.CompilerParams(vmem_limit_bytes=56 * 1024 * 1024),
        cost_estimate=pl.CostEstimate(
            flops=12 * count * dim * hidden,
            bytes_accessed=6 * dim * hidden + 8 * count * dim,
            transcendentals=count * hidden,
        ),
        name="shared_rows",
    )(rows, grads, weights)


def shared_grads_kernel(rows, grads, d_gate, d_up, hidden, out):
    number = pl.program_id(0)

    def write(left, right):
        out[...] = contract_first(left[...], right[...]).astype(bf16).reshape(out.shape)

    pl.when(number == 0)(lambda: write(rows, d_gate))
    pl.when(number == 1)(lambda: write(rows, d_up))
    pl.when(number == 2)(lambda: write(grads, hidden))


def shared_grads(rows, grads, d_gate, d_up, hidden, own_rows):
    count, dim = rows.shape
    width = d_gate.shape[1]
    wide = pl.BlockSpec((count, dim), lambda i: (0, 0))
    narrow = pl.BlockSpec((count, width), lambda i: (0, 0))
    return pl.pallas_call(
        shared_grads_kernel,
        out_shape=jax.ShapeDtypeStruct((FSDP, 3, own_rows, width), bf16),
        grid=(3,),
        in_specs=[wide] * 2 + [narrow] * 3,
        out_specs=pl.BlockSpec((FSDP, 1, own_rows, width), lambda i: (0, i, 0, 0)),
        compiler_params=pltpu.CompilerParams(vmem_limit_bytes=48 * 1024 * 1024),
        cost_estimate=pl.CostEstimate(
            flops=6 * count * dim * width,
            bytes_accessed=6 * dim * width + 4 * count * dim,
            transcendentals=0,
        ),
        name="shared_grads",
    )(rows, grads, d_gate, d_up, hidden)


def attention_grads_kernel(spot, d_att, attended, rows, logits, gains, gain_lane, h_attn, d_qkv, *refs):
    for_z, for_y, whole = refs[:NZ], refs[NZ : NZ + NY], refs[-1]
    wide = attended.shape[1]

    def put(start, value):
        shape = (*whole.shape[:-1], value.shape[1])
        whole[..., start : start + value.shape[1]] = value.astype(bf16).reshape(shape)

    put(0, contract_first(d_att[...], attended[...]))
    put(wide, contract_first(rows[...], logits[...]) + contract_first(gains[...], gain_lane[...]))
    put(wide + LANES, contract_first(h_attn[...], d_qkv[...]))
    write_pieces(spot, whole, 0, for_z, for_y)


def attention_grads(spot, *args):
    d_att, attended, d_qkv = args[0], args[1], args[-1]
    count, dim = d_att.shape
    half = dim // FSDP // 2
    width = attended.shape[1] + LANES + d_qkv.shape[1]
    shapes = piece_shapes(1, half, width)
    outs = pl.pallas_call(
        attention_grads_kernel,
        out_shape=shapes,
        in_specs=[pl.BlockSpec(memory_space=pltpu.SMEM)]
        + [pl.BlockSpec(memory_space=pltpu.VMEM)] * len(args),
        out_specs=[pl.BlockSpec(memory_space=pltpu.VMEM)] * len(shapes),
        scratch_shapes=[pltpu.VMEM((NZ, NX, NY, 2, half, width), bf16)],
        compiler_params=pltpu.CompilerParams(vmem_limit_bytes=48 * 1024 * 1024),
        cost_estimate=pl.CostEstimate(
            flops=2 * count * dim * width,
            bytes_accessed=2 * dim * width + 8 * count * dim,
            transcendentals=0,
        ),
        name="attention_grads",
    )(spot, *args)
    return outs[:NZ], outs[NZ:]


def expert_grads_kernel(core, rows_own, rows_far, grads_own, grads_far, d_gate, d_up, scaled, *outs):
    half = pl.program_id(0)

    def write(rows, grads):
        outs[0][...] = contract_first(d_gate[...], rows[...])
        outs[1][...] = contract_first(d_up[...], rows[...])
        outs[2][...] = contract_first(scaled[...], grads[...])

    pl.when(half == 0)(lambda: write(rows_own, grads_own))
    pl.when(half == 1)(lambda: write(rows_far, grads_far))


def expert_grads(core, rows_own, rows_far, grads_own, grads_far, d_gate, d_up, scaled):
    rows, wide = grads_own.shape
    hidden = d_gate.shape[1]
    full = pl.BlockSpec((rows, wide), lambda h, c: (0, 0))
    part = pl.BlockSpec((rows, hidden), lambda h, c: (0, 0))
    result = pl.BlockSpec((hidden, wide), lambda h, c: (0, jnp.bitwise_xor(h, c[0])))
    return pl.pallas_call(
        expert_grads_kernel,
        out_shape=[jax.ShapeDtypeStruct((hidden, 2 * wide), f32)] * 3,
        grid_spec=pltpu.PrefetchScalarGridSpec(
            num_scalar_prefetch=1,
            grid=(2,),
            in_specs=[full] * 4 + [part] * 3,
            out_specs=[result] * 3,
        ),
        compiler_params=pltpu.CompilerParams(vmem_limit_bytes=56 * 1024 * 1024),
        cost_estimate=pl.CostEstimate(
            flops=12 * rows * wide * hidden,
            bytes_accessed=24 * hidden * wide + 12 * rows * wide,
            transcendentals=0,
        ),
        name="expert_grads",
    )(core, rows_own, rows_far, grads_own, grads_far, d_gate, d_up, scaled)


def per_device(
    tokens,
    g_attn,
    query_matrix,
    key_matrix,
    value_matrix,
    w_out,
    g_ffn,
    w_router,
    shared_gate,
    shared_up,
    shared_down,
    expert_gate,
    expert_up,
    expert_down,
    lengths,
    routes,
    cotangent,
):
    tok_dev, dim = tokens.shape
    group_rows = tok_dev * TP
    near = group_rows // 2
    experts = w_router.shape[1]
    own_rows = w_router.shape[0]
    q_width, kv_width = query_matrix.shape[1], key_matrix.shape[1]
    qkv_width = q_width + 2 * kv_width
    heads = q_width // HEAD_SIZE
    local_experts, _, hidden_own = expert_gate.shape
    half_dim = dim // 2
    fsdp_at = lax.axis_index("fsdp")
    rank = lax.axis_index("tp")
    core = lax.rem(rank, 2)
    core_vec = core.astype(jnp.int32).reshape(1)
    spot = jnp.stack(
        [fsdp_at // (NX * NY), lax.rem(fsdp_at // NY, NX), lax.rem(fsdp_at, NY)]
    ).astype(jnp.int32)

    route_blocks = routes.reshape(TP, tok_dev, routes.shape[1])
    own_routes = jnp.concatenate(
        [pick(route_blocks, jnp.bitwise_xor(b, rank), 0) for b in BLOCK_ORDER], axis=0
    )
    places = jnp.concatenate(
        [jnp.bitwise_xor(b, rank) * tok_dev + jnp.arange(tok_dev) for b in BLOCK_ORDER]
    ).astype(jnp.int32)
    expert_lane = jnp.arange(LANES, dtype=jnp.int32)[None, :]
    hot = (own_routes[:, 0:1] == expert_lane) | (own_routes[:, 1:2] == expert_lane)
    before = (places[None, :] < places[:, None]).astype(bf16)
    earlier = matmul(before, hot.astype(bf16))
    slots = experts * CAP
    slot_ids = jnp.arange(slots, dtype=jnp.int32)
    spread = (slot_ids[None, :] // CAP == jnp.arange(LANES, dtype=jnp.int32)[:, None]).astype(bf16)
    slot_wanted = matmul(jnp.where(hot, earlier, -1.0).astype(bf16), spread)
    dispatch = (slot_wanted == (slot_ids % CAP).astype(f32)[None, :]).astype(bf16)

    def core_half(values):
        return lax.dynamic_slice_in_dim(values, core * half_dim, half_dim, 1)

    small_tile = jnp.concatenate(
        [
            w_router,
            g_attn[:, None],
            g_ffn[:, None],
            jnp.zeros((own_rows, LANES - experts - 2), bf16),
        ],
        axis=1,
    )
    qkv_own = jnp.concatenate([query_matrix, key_matrix, value_matrix], axis=1)
    pair = gather_pair(jnp.concatenate([qkv_own, small_tile, w_out], axis=1)[None])
    grad_other = move_tp(cotangent, 2)
    *lines, grad_other = lax.optimization_barrier((*gather_lines(pair), grad_other))
    grad_pair = jnp.concatenate([cotangent, grad_other], axis=0)
    near_lines = gather_near(lines)
    grad_rows = jnp.concatenate([grad_pair, move_tp(grad_pair, 1)], axis=0)
    token_pair = jnp.concatenate([tokens, after(move_tp(tokens, 2), *near_lines)], axis=0)
    token_rows = jnp.concatenate([token_pair, move_tp(token_pair, 1)], axis=0)
    w_qkv, w_tile, w_out_all = gather_all(
        lines,
        near_lines,
        spot,
        (
            (0, 0, qkv_width),
            (0, qkv_width, LANES),
            (0, qkv_width + LANES, q_width),
        ),
    )
    slot_grads = contract_first(dispatch, core_half(grad_rows)).astype(bf16)
    grads_own = swap_fsdp(after(slot_grads, w_tile))
    shared_own = jnp.concatenate([shared_gate, shared_up, shared_down], axis=0)
    w_shared = lax.all_gather(
        shared_own, "fsdp", axis=0, tiled=True
    ).reshape(FSDP, 3, own_rows, shared_gate.shape[1])
    lane = lax.broadcasted_iota(jnp.int32, (8, LANES), 1)
    gain_pick = (lane == experts + lax.broadcasted_iota(jnp.int32, (8, LANES), 0)).astype(bf16)
    gains = contract_last(gain_pick, w_tile)
    gain_one, gain_two = gains[0:1], gains[1:2]

    hidden_all = local_experts * hidden_own

    def by_hidden(weights):
        return jnp.swapaxes(weights, 1, 2).reshape(hidden_all, dim)

    gate_w, up_w, down_w = by_hidden(expert_gate), by_hidden(expert_up), by_hidden(expert_down)

    ends = jnp.cumsum(lengths[0])
    where = jnp.stack([rank.astype(jnp.int32), ends[0], ends[1]]).astype(jnp.int32)
    normed_one, _ = norm_rows(token_rows.astype(f32), gain_one)
    h_attn = normed_one.astype(bf16)
    qkv = matmul(h_attn, w_qkv).astype(bf16)
    attended = attend(where, qkv, heads)
    attn_far = after(contract_last(attended[near:], w_out_all).astype(bf16), grads_own)
    attn_own = sum_chips(sum_cores(contract_last(attended[:near], w_out_all), attn_far))
    own_tokens = tokens.astype(f32)
    middle = own_tokens + attn_own
    normed_two, factor_two = norm_rows(middle, gain_two)
    h_ffn = gather_tp(normed_two.astype(bf16))

    logits = matmul(h_ffn, w_tile)
    top = jnp.max(jnp.where(hot, logits, -1e30), axis=-1, keepdims=True)
    gate_exp = jnp.where(hot, jnp.exp(jnp.minimum(logits - top, 0.0)), 0.0)
    gates = gate_exp / jnp.sum(gate_exp, axis=-1, keepdims=True)
    gate_high = gates.astype(bf16)
    gate_low = (gates - gate_high.astype(f32)).astype(bf16)
    gate_lanes = jnp.concatenate([gate_high[:, :experts], gate_low[:, :experts]], axis=1)

    slot_rows = contract_first(
        dispatch, jnp.concatenate([core_half(h_ffn), gate_lanes], axis=1)
    ).astype(bf16)
    grads_far = move_tp(after(grads_own, slot_rows), 1)
    rows_own = swap_fsdp(slot_rows)

    h_then = after(h_ffn, slot_rows)
    s_d_gate, s_d_up, s_hidden, shared_out, shared_back = shared_rows(h_then, grad_rows, w_shared)
    shared_parts = shared_grads(h_then, grad_rows, s_d_gate, s_d_up, s_hidden, own_rows)
    shared_lines = sum_along_z(shared_parts)

    rows_own = after(rows_own, shared_back, shared_parts)

    rows_far = move_tp(rows_own, 1)
    scal = jnp.stack([core.astype(jnp.int32), local_experts * fsdp_at.astype(jnp.int32)])
    d_gate, d_up, hidden, sent_far, dot_lanes = expert_rows(
        scal, rows_own, rows_far, grads_own, grads_far, gate_w, up_w, down_w
    )
    sent_far = move_tp(sent_far, 1)
    sent_own = (matmul(d_gate, core_half(gate_w)) + matmul(d_up, core_half(up_w))).astype(bf16)
    payload = add_and_join(sent_own, sent_far, dot_lanes)
    returned = swap_fsdp(payload)

    hidden_then = after(hidden, payload)
    grad_egate, grad_eup, grad_edown = expert_grads(
        core_vec, rows_own, rows_far, grads_own, grads_far, d_gate, d_up, hidden_then
    )
    down_own = core_half(down_w)
    down_far = lax.dynamic_slice_in_dim(down_w, (1 - core) * half_dim, half_dim, 1)
    out_far = move_tp(matmul(hidden_then, down_far).astype(bf16), 1)
    out_own = (matmul(hidden_then, down_own) + out_far.astype(f32)).astype(bf16)

    def expert_layout(grads):
        return jnp.swapaxes(grads.reshape(local_experts, hidden_own, dim), 1, 2)

    returned = after(returned, out_own, grad_egate)
    ffn_far, logits_far = combine(
        core_vec, 1, dispatch, returned, shared_back, bf16, gates, w_tile
    )
    ffn_near, logits_near = combine(
        core_vec, 0, dispatch, returned, shared_back, f32, gates, w_tile
    )
    d_h_ffn = sum_chips(sum_cores(ffn_near, ffn_far))
    d_middle = cotangent.astype(f32) + norm_back(middle, factor_two, gain_two, d_h_ffn)
    lane_ids = lax.broadcasted_iota(jnp.int32, (1, LANES), 1)
    gain_terms = (d_h_ffn * middle * factor_two).astype(bf16)
    gain_lane = jnp.broadcast_to(lane_ids == experts, (tok_dev, LANES)).astype(bf16)
    d_att_own = d_middle.astype(bf16)
    d_att_near = jnp.concatenate([d_att_own, move_tp(d_att_own, 2)], axis=0)
    out_back = swap_fsdp(after(out_own, d_att_near))
    d_att = jnp.concatenate([d_att_near, move_tp(d_att_near, 1)], axis=0)

    d_attended = matmul(after(d_att, shared_lines), w_out_all).astype(bf16)
    d_qkv = attend_back(where, qkv, d_attended, heads)
    grad_pieces = attention_grads(
        spot,
        d_att,
        attended,
        h_ffn,
        jnp.concatenate([logits_near, logits_far], axis=0),
        gain_terms,
        gain_lane,
        h_attn,
        d_qkv,
    )
    grad_received = trade_pieces(grad_pieces)
    sum_parts = add_pieces(grad_pieces[0][0], grad_pieces[1][0], grad_received)
    first_part = grad_received[0][0]
    d_qkv_then = after(d_qkv, first_part)
    attn_far = contract_last(d_qkv_then[near:], w_qkv).astype(bf16)
    d_h_half = sum_cores(contract_last(d_qkv_then[:near], w_qkv), attn_far)
    back_then = after(out_back, first_part)
    (out_far,) = combine(core_vec, 1, dispatch, back_then, shared_out, bf16)
    (out_near,) = combine(core_vec, 0, dispatch, back_then, shared_out, f32)
    out_half = sum_cores(out_near, out_far)
    shared_sums = sum_across(after(shared_lines, first_part))
    sum_parts = lax.optimization_barrier((*sum_parts, d_h_half, out_half))[:2]
    d_h_attn = sum_chips(d_h_half)
    output = (middle + sum_chips(out_half)).astype(bf16)
    sums = scatter_fsdp_two(sum_parts, spot)[0]
    out_sums, tile_sums = sums[:, :q_width], small_sum_tp(sums[:, q_width : q_width + LANES])
    qkv_sums = sums[:, q_width + LANES :]
    _, factor_one = norm_rows(own_tokens, gain_one)
    grad_tokens = (d_middle + norm_back(own_tokens, factor_one, gain_one, d_h_attn)).astype(bf16)
    gain_sum = jnp.sum(qkv_sums * qkv_own.astype(f32), axis=1)
    grad_g_attn = small_sum_tp(gain_sum) / g_attn.astype(f32)
    return (
        output,
        grad_tokens,
        grad_g_attn,
        qkv_sums[:, :q_width],
        qkv_sums[:, q_width : q_width + kv_width],
        qkv_sums[:, q_width + kv_width :],
        out_sums,
        tile_sums[:, experts],
        tile_sums[:, :experts],
        shared_sums[0],
        shared_sums[1],
        shared_sums[2],
        expert_layout(grad_egate),
        expert_layout(grad_eup),
        expert_layout(grad_edown),
    )


def solution(mesh):
    in_specs = (
        P(("fsdp", "tp"), None),
        P("fsdp"),
        P("fsdp", "tp"),
        P("fsdp", "tp"),
        P("fsdp", "tp"),
        P("fsdp", "tp"),
        P("fsdp"),
        P("fsdp", None),
        P("fsdp", "tp"),
        P("fsdp", "tp"),
        P("fsdp", "tp"),
        P("fsdp", None, "tp"),
        P("fsdp", None, "tp"),
        P("fsdp", None, "tp"),
        P("fsdp", None),
        P("fsdp", None),
        P(("fsdp", "tp"), None),
    )
    out_specs = (
        P(("fsdp", "tp"), None),
        P(("fsdp", "tp"), None),
        P("fsdp"),
        P("fsdp", "tp"),
        P("fsdp", "tp"),
        P("fsdp", "tp"),
        P("fsdp", "tp"),
        P("fsdp"),
        P("fsdp", None),
        P("fsdp", "tp"),
        P("fsdp", "tp"),
        P("fsdp", "tp"),
        P("fsdp", None, "tp"),
        P("fsdp", None, "tp"),
        P("fsdp", None, "tp"),
    )
    return jax.shard_map(
        per_device, mesh=mesh, in_specs=in_specs, out_specs=out_specs, check_vma=False
    )
```

```python
import functools

import jax
import jax.numpy as jnp
from jax import lax
from jax.experimental import pallas as pl
from jax.experimental.pallas import tpu as pltpu
from jax.sharding import PartitionSpec as P

HEAD_SIZE = 128
NZ, NX, NY = 4, 2, 4
FSDP = NZ * NX * NY
TP = 4
CAP = 20
LANES = 128
BLOCK_ORDER = (0, 2, 1, 3)
bf16 = jnp.bfloat16
f32 = jnp.float32

epsilon = 1e-06


def contract_first(left_op, right_op):
    return lax.dot_general(
        left_op, right_op, (((0,), (0,)), ((), ())), preferred_element_type=f32
    )


def contract_last(left_op, right_op):
    return lax.dot_general(
        left_op, right_op, (((1,), (1,)), ((), ())), preferred_element_type=f32
    )


def matmul(left_op, right_op):
    return jnp.dot(left_op, right_op, preferred_element_type=f32)


def norm_rows(values, gain_vec):
    factor = lax.rsqrt(jnp.mean(values * values, axis=-1, keepdims=True) + epsilon)
    return (values * factor * gain_vec, factor)


def norm_back(values, factor, gain_vec, upstream):
    scaled_up = upstream * gain_vec
    return factor * scaled_up - values * factor * factor * factor * jnp.mean(
        scaled_up * values, axis=-1, keepdims=True
    )


def after(value, *earlier):
    return lax.optimization_barrier((value, *earlier))[0]


def swap_along(values, fz, fx, fy):
    return route_fsdp(values, lambda z, x, y: (z ^ fz, x ^ fx, y ^ fy))


def route_fsdp(values, target):
    pairs = []
    for z in range(NZ):
        for x in range(NX):
            for y in range(NY):
                to_z, to_x, to_y = target(z, x, y)
                pairs.append(((z * NX + x) * NY + y, (to_z * NX + to_x) * NY + to_y))
    return lax.ppermute(values, "fsdp", pairs)


def move_tp(values, flip):
    return lax.ppermute(values, "tp", [(i, i ^ flip) for i in range(TP)])


def gather_tp(own):
    pair = jnp.concatenate([own, move_tp(own, 2)], axis=0)
    return jnp.concatenate([pair, move_tp(pair, 1)], axis=0)


def sum_cores(near_part, far_part):
    return near_part + move_tp(far_part.astype(bf16), 1).astype(f32)


def sum_chips(summed):
    rows = summed.shape[0] // 2
    return summed[:rows] + move_tp(summed[rows:].astype(bf16), 2).astype(f32)


def small_sum_tp(values):
    return values + move_tp(values, 1) + move_tp(values, 2) + move_tp(values, 3)


def swap_fsdp(values):
    shape = values.shape
    blocks = values.reshape(FSDP, shape[0] // FSDP, shape[1])
    return lax.all_to_all(blocks, "fsdp", split_axis=0, concat_axis=0, tiled=True).reshape(shape)


def sum_along_z(values):
    lines = [[z * NX * NY + i for z in range(NZ)] for i in range(NX * NY)]
    return lax.psum_scatter(
        values, "fsdp", scatter_dimension=0, tiled=True, axis_index_groups=lines
    )


def sum_across(values):
    planes = [[z * NX * NY + i for i in range(NX * NY)] for z in range(NZ)]
    parts = lax.all_to_all(
        values, "fsdp", split_axis=0, concat_axis=0, tiled=True, axis_index_groups=planes
    )
    return jnp.sum(parts.astype(f32), axis=0)


def place_kernel(cuts, spot, *refs):
    pieces, outs, held, sems = refs[:10], refs[10 : 10 + len(cuts)], refs[-11:-1], refs[-1]
    z, x, y = spot[0], spot[1], spot[2]
    half = pieces[0].shape[3]
    copies = [pltpu.make_async_copy(pieces[i], held[i], sems.at[i]) for i in range(10)]
    for copy in copies:
        copy.start()
    for number in range(10):
        copies[number].wait()
        lines, across = divmod(number, 5)
        opposite = across in (2, 3)
        for place in range(held[number].shape[0]):
            along_line = place + 2 * (across == 3)
            step = 2 if opposite else (0, 1, 2, 2, 3)[across]
            zr, yr = (step, along_line) if lines == 0 else (along_line, step)
            rows = slice(lines * half, (lines + 1) * half)
            for xr in range(NX):
                at = (jnp.bitwise_xor(z, zr), jnp.bitwise_xor(x, xr), jnp.bitwise_xor(y, yr))
                for out, (item, start, width) in zip(outs, cuts):
                    out[at[0], at[1], at[2], rows] = held[number][
                        place, xr, item, :, start : start + width
                    ]


def gather_pair(stacked):
    half = stacked.shape[1] // 2
    pair = jnp.stack([stacked, swap_along(stacked, 0, 1, 0)])
    return pair[:, :, :half], pair[:, :, half:]


def gather_lines(pair):
    near_y, near_z = pair
    by_y = jnp.stack([near_y] + [swap_along(near_y, 0, 0, r) for r in range(1, NY)])
    by_z = jnp.stack([near_z] + [swap_along(near_z, r, 0, 0) for r in range(1, NZ)])
    return lax.optimization_barrier((by_y, by_z))


def gather_near(lines):
    by_y, by_z = lines
    return lax.optimization_barrier(
        (
            swap_along(by_y, 1, 0, 0),
            swap_along(by_y, 3, 0, 0),
            swap_along(by_z, 0, 0, 1),
            swap_along(by_z, 0, 0, 3),
        )
    )


def gather_all(lines, near, spot, cuts):
    by_y, by_z = lines
    rows = 2 * by_y.shape[3]
    first = [by_y, near[0], swap_along(near[0][:2], 3, 0, 0), swap_along(near[1][2:], 1, 0, 0), near[1]]
    second = [by_z, near[2], swap_along(near[2][:2], 0, 0, 3), swap_along(near[3][2:], 0, 0, 1), near[3]]
    total = FSDP * rows
    wholes = pl.pallas_call(
        functools.partial(place_kernel, cuts),
        out_shape=[jax.ShapeDtypeStruct((NZ, NX, NY, rows, width), bf16) for _, _, width in cuts],
        in_specs=[pl.BlockSpec(memory_space=pltpu.SMEM)]
        + [pl.BlockSpec(memory_space=pl.ANY)] * 10,
        out_specs=[pl.BlockSpec(memory_space=pltpu.VMEM)] * len(cuts),
        scratch_shapes=[pltpu.VMEM(piece.shape, bf16) for piece in first + second]
        + [pltpu.SemaphoreType.DMA((10,))],
        compiler_params=pltpu.CompilerParams(vmem_limit_bytes=60 * 1024 * 1024),
        cost_estimate=pl.CostEstimate(
            flops=0, bytes_accessed=4 * total * sum(w for _, _, w in cuts), transcendentals=0
        ),
        name="place",
    )(spot, *first, *second)
    return [whole.reshape(total, width) for whole, (_, _, width) in zip(wholes, cuts)]


def pick(values, index, axis):
    return lax.dynamic_index_in_dim(values, index, axis, keepdims=False)


def add_up(own, received):
    total = own.astype(f32)
    for part in received:
        total = total + part.astype(f32)
    return total.astype(bf16)


def trade_pieces(pieces):
    for_z, for_y = pieces
    near = [swap_along(for_z[1], 1, 0, 0), swap_along(for_z[3], 3, 0, 0)]
    across = [swap_along(for_y[1], 0, 0, 1), swap_along(for_y[3], 0, 0, 3)]
    near.append(swap_along(for_z[2], 2, 0, 0))
    across.append(swap_along(for_y[2], 0, 0, 2))
    return near, across


def add_pieces(own_z, own_y, received):
    return lax.optimization_barrier((add_up(own_z, received[0]), add_up(own_y, received[1])))


def write_pieces(spot, whole, item, for_z, for_y):
    for r in range(NZ):
        for_z[r][item] = whole[jnp.bitwise_xor(spot[0], r), :, :, 0]
    for r in range(NY):
        for_y[r][item] = whole[:, :, jnp.bitwise_xor(spot[2], r), 1]


def piece_shapes(items, half, columns):
    return [jax.ShapeDtypeStruct((items, NX, NY, half, columns), bf16)] * NZ + [
        jax.ShapeDtypeStruct((items, NZ, NX, half, columns), bf16)
    ] * NY


def scatter_fsdp_two(parts, spot):
    z, x, y = spot[0], spot[1], spot[2]
    halves = (
        [pick(parts[0], jnp.bitwise_xor(y, r), 2) for r in range(NY)],
        [pick(parts[1], jnp.bitwise_xor(z, r), 1) for r in range(NZ)],
    )
    in_z, in_y = trade_pieces((halves[1], halves[0]))
    one, two = lax.optimization_barrier((add_up(halves[0][0], in_y), add_up(halves[1][0], in_z)))

    def last_sum(kept):
        mine, theirs = pick(kept, x, 1), pick(kept, 1 - x, 1)
        return mine.astype(f32) + swap_along(theirs, 0, 1, 0).astype(f32)

    return jnp.concatenate([last_sum(one), last_sum(two)], axis=1)


def fill_bias(where, bias):
    size = bias.shape[0]
    rank, end_one, end_two = where[0], where[1], where[2]

    def place_of(index):
        block = lax.div(index, LANES)
        block = 2 * lax.rem(block, 2) + lax.div(block, 2)
        return jnp.bitwise_xor(block, rank) * LANES + lax.rem(index, LANES)

    queries = place_of(lax.broadcasted_iota(jnp.int32, (size, 1), 0))
    keys = place_of(lax.broadcasted_iota(jnp.int32, (1, size), 1))
    start = jnp.where(queries >= end_two, end_two, jnp.where(queries >= end_one, end_one, 0))
    visible = (keys <= queries) & (keys >= start)
    bias[...] = jnp.where(visible, 0.0, -1e30).astype(f32)


def exponents(q_ref, k_ref, bias):
    scores = contract_last(q_ref[...], k_ref[...]) * (HEAD_SIZE**-0.5) + bias[...]
    exponent = jnp.exp(scores - jnp.max(scores, axis=-1, keepdims=True))
    return exponent / jnp.sum(exponent, axis=-1, keepdims=True)


def attend_kernel(where, q_ref, k_ref, v_ref, out_ref, bias):
    @pl.when(pl.program_id(0) == 0)
    def _():
        fill_bias(where, bias)

    probability = exponents(q_ref, k_ref, bias).astype(bf16)
    out_ref[...] = matmul(probability, v_ref[...]).astype(bf16)


def attend(where, qkv, heads):
    rows = qkv.shape[0]
    block = (rows, HEAD_SIZE)
    return pl.pallas_call(
        attend_kernel,
        out_shape=jax.ShapeDtypeStruct((rows, heads * HEAD_SIZE), bf16),
        grid_spec=pltpu.PrefetchScalarGridSpec(
            num_scalar_prefetch=1,
            grid=(heads,),
            in_specs=[
                pl.BlockSpec(block, lambda h, w: (0, h)),
                pl.BlockSpec(block, lambda h, w: (0, heads)),
                pl.BlockSpec(block, lambda h, w: (0, heads + 1)),
            ],
            out_specs=pl.BlockSpec(block, lambda h, w: (0, h)),
            scratch_shapes=[pltpu.VMEM((rows, rows), f32)],
        ),
        compiler_params=pltpu.CompilerParams(vmem_limit_bytes=40 * 1024 * 1024),
        cost_estimate=pl.CostEstimate(
            flops=4 * heads * rows * rows * HEAD_SIZE,
            bytes_accessed=4 * rows * heads * HEAD_SIZE,
            transcendentals=heads * rows * rows,
        ),
        name="attend",
    )(where, qkv, qkv, qkv)


def attend_back_kernel(heads, where, q_ref, k_ref, v_ref, g_ref, out_ref, bias, key_sum, value_sum):
    head = pl.program_id(0)

    @pl.when(head == 0)
    def _():
        fill_bias(where, bias)
        key_sum[...] = jnp.zeros_like(key_sum)
        value_sum[...] = jnp.zeros_like(value_sum)

    scale = HEAD_SIZE**-0.5
    probability = exponents(q_ref, k_ref, bias)
    grad_prob = contract_last(g_ref[...], v_ref[...])
    inner = jnp.sum(probability * grad_prob, axis=-1, keepdims=True)
    grad_scores = (probability * (grad_prob - inner)).astype(bf16)
    columns = pl.ds(pl.multiple_of(head * HEAD_SIZE, HEAD_SIZE), HEAD_SIZE)
    out_ref[:, columns] = (matmul(grad_scores, k_ref[...]) * scale).astype(bf16)
    key_sum[...] += contract_first(grad_scores, q_ref[...])
    value_sum[...] += contract_first(probability.astype(bf16), g_ref[...])

    @pl.when(head == heads - 1)
    def _():
        wide = heads * HEAD_SIZE
        out_ref[:, wide : wide + HEAD_SIZE] = (key_sum[...] * scale).astype(bf16)
        out_ref[:, wide + HEAD_SIZE :] = value_sum[...].astype(bf16)


def attend_back(where, qkv, grads, heads):
    rows = qkv.shape[0]
    block = (rows, HEAD_SIZE)
    return pl.pallas_call(
        functools.partial(attend_back_kernel, heads),
        out_shape=jax.ShapeDtypeStruct(qkv.shape, bf16),
        grid_spec=pltpu.PrefetchScalarGridSpec(
            num_scalar_prefetch=1,
            grid=(heads,),
            in_specs=[
                pl.BlockSpec(block, lambda h, w: (0, h)),
                pl.BlockSpec(block, lambda h, w: (0, heads)),
                pl.BlockSpec(block, lambda h, w: (0, heads + 1)),
                pl.BlockSpec(block, lambda h, w: (0, h)),
            ],
            out_specs=pl.BlockSpec(qkv.shape, lambda h, w: (0, 0)),
            scratch_shapes=[
                pltpu.VMEM((rows, rows), f32),
                pltpu.VMEM(block, f32),
                pltpu.VMEM(block, f32),
            ],
        ),
        compiler_params=pltpu.CompilerParams(vmem_limit_bytes=40 * 1024 * 1024),
        cost_estimate=pl.CostEstimate(
            flops=10 * heads * rows * rows * HEAD_SIZE,
            bytes_accessed=6 * rows * heads * HEAD_SIZE,
            transcendentals=heads * rows * rows,
        ),
        name="attend_back",
    )(where, qkv, qkv, qkv, grads)


def expert_rows_kernel(
    scal, rows_own, gate_lanes, rows_far, grads_own, grads_far,
    eg_own, eg_far, eu_own, eu_far, ed_own, ed_far, d_gate, d_up, hidden, sent_far, dots,
):
    count, width = rows_own.shape[0], eg_own.shape[0]
    experts = dots.shape[1] // 2
    row = lax.broadcasted_iota(jnp.int32, (count, 1), 0) + pl.program_id(0) * count
    second = (lax.rem(row, 2 * CAP) >= CAP).astype(jnp.int32)
    column = (lax.broadcasted_iota(jnp.int32, (1, width), 1) >= width // 2).astype(jnp.int32)
    mine = second == column
    lane = lax.broadcasted_iota(jnp.int32, (1, 2 * experts), 1)
    expert_of = scal[1] + second
    high_lane, low_lane = lane == expert_of, lane == experts + expert_of
    gate_of = jnp.sum(
        jnp.where(high_lane | low_lane, gate_lanes[...].astype(f32), 0.0), axis=1, keepdims=True
    )
    gate_mine = jnp.where(mine, gate_of, 0.0)

    def product(own, far, w_own, w_far):
        return contract_last(own[...], w_own[...]) + contract_last(far[...], w_far[...])

    gate_pre = product(rows_own, rows_far, eg_own, eg_far)
    up_pre = product(rows_own, rows_far, eu_own, eu_far)
    down_back = product(grads_own, grads_far, ed_own, ed_far) * gate_mine
    sigmoid_v = 0.5 + 0.5 * jnp.tanh(0.5 * gate_pre)
    silu_gate = gate_pre * sigmoid_v
    hidden_wide = silu_gate * up_pre
    hidden[...] = (hidden_wide * gate_mine).astype(bf16)
    gate_part = (
        down_back * up_pre * (sigmoid_v * (1.0 + gate_pre * (1.0 - sigmoid_v)))
    ).astype(bf16)
    up_part = (down_back * silu_gate).astype(bf16)
    d_gate[...] = gate_part
    d_up[...] = up_part
    sent_far[...] = (matmul(gate_part, eg_far[...]) + matmul(up_part, eu_far[...])).astype(bf16)
    slot_dot = jnp.sum(hidden_wide * down_back, axis=1, keepdims=True)
    high = slot_dot.astype(bf16).astype(f32)
    dots[...] = jnp.where(high_lane, high, jnp.where(low_lane, slot_dot - high, 0.0)).astype(bf16)


def expert_rows(scal, rows_own, rows_far, grads_own, grads_far, gate_w, up_w, down_w, steps=2):
    rows, wide = grads_own.shape
    hidden = gate_w.shape[0]
    count = rows // steps
    block = pl.BlockSpec((count, wide), lambda i, c: (i, 0))
    own = pl.BlockSpec((hidden, wide), lambda i, c: (0, c[0]))
    far = pl.BlockSpec((hidden, wide), lambda i, c: (0, 1 - c[0]))
    narrow = pl.BlockSpec((count, hidden), lambda i, c: (i, 0))
    lanes = pl.BlockSpec((count, LANES), lambda i, c: (i, 0))
    last_lanes = pl.BlockSpec((count, LANES), lambda i, c: (i, wide // LANES))
    shape = lambda columns: jax.ShapeDtypeStruct((rows, columns), bf16)
    return pl.pallas_call(
        expert_rows_kernel,
        out_shape=[shape(hidden), shape(hidden), shape(hidden), shape(wide), shape(LANES)],
        grid_spec=pltpu.PrefetchScalarGridSpec(
            num_scalar_prefetch=1,
            grid=(steps,),
            in_specs=[block, last_lanes] + [block] * 3 + [own, far] * 3,
            out_specs=[narrow] * 3 + [block, lanes],
        ),
        compiler_params=pltpu.CompilerParams(vmem_limit_bytes=56 * 1024 * 1024),
        cost_estimate=pl.CostEstimate(
            flops=16 * rows * wide * hidden,
            bytes_accessed=12 * hidden * wide + 12 * rows * wide,
            transcendentals=rows * hidden,
        ),
        name="expert_rows",
    )(
        scal, rows_own, rows_own, rows_far, grads_own, grads_far,
        gate_w, gate_w, up_w, up_w, down_w, down_w,
    )


def join_kernel(left, right, tail, out):
    wide = left.shape[1]
    out[:, :wide] = (left[...].astype(f32) + right[...].astype(f32)).astype(bf16)
    out[:, wide:] = tail[...]


def add_and_join(left, right, tail, steps=4):
    rows, wide = left.shape
    block = pl.BlockSpec((rows // steps, wide), lambda i: (i, 0))
    return pl.pallas_call(
        join_kernel,
        out_shape=jax.ShapeDtypeStruct((rows, wide + tail.shape[1]), bf16),
        grid=(steps,),
        in_specs=[block, block, pl.BlockSpec((rows // steps, tail.shape[1]), lambda i: (i, 0))],
        out_specs=pl.BlockSpec((rows // steps, wide + tail.shape[1]), lambda i: (i, 0)),
        cost_estimate=pl.CostEstimate(
            flops=rows * wide, bytes_accessed=6 * rows * wide, transcendentals=0
        ),
        name="add_and_join",
    )(left, right, tail)


def combine_kernel(with_logits, core, dispatch, back, base, *refs):
    half = base.shape[1] // 2
    total = matmul(dispatch[...], back[...])
    extra = 0.0
    if with_logits:
        gates, tile, out, logits = refs
        experts = LANES // 2
        lanes = total[:, half:]
        dots = lanes + pltpu.roll(lanes, experts, 1)
        lane = lax.broadcasted_iota(jnp.int32, dots.shape, 1)
        dots = jnp.where(lane < experts, dots, 0.0)
        d_logits = (dots - gates[...] * jnp.sum(dots, axis=-1, keepdims=True)).astype(bf16)
        logits[...] = d_logits
        extra = contract_last(d_logits, tile[...])
    else:
        (out,) = refs
    sums = base[...].astype(f32) + extra
    for number in range(2):
        columns = slice(number * half, (number + 1) * half)
        chosen = jnp.where(core[0] == number, total[:, :half], 0.0)
        out[:, columns] = (sums[:, columns] + chosen).astype(out.dtype)


def combine(core, block, dispatch, back, base, dtype, gates=None, tile=None):
    rows, dim = base.shape[0] // 2, base.shape[1]
    slots, width = back.shape
    with_logits = gates is not None
    part = lambda columns: pl.BlockSpec((rows, columns), lambda i, c: (block, 0))
    whole = lambda shape: pl.BlockSpec(shape, lambda i, c: (0, 0))
    specs = [part(slots), whole((slots, width)), part(dim)]
    args = [dispatch, back, base]
    shapes = [jax.ShapeDtypeStruct((rows, dim), dtype)]
    outs = [whole((rows, dim))]
    if with_logits:
        specs += [part(LANES), whole(tile.shape)]
        args += [gates, tile]
        shapes.append(jax.ShapeDtypeStruct((rows, LANES), bf16))
        outs.append(whole((rows, LANES)))
    return pl.pallas_call(
        functools.partial(combine_kernel, with_logits),
        out_shape=shapes,
        grid_spec=pltpu.PrefetchScalarGridSpec(
            num_scalar_prefetch=1, grid=(1,), in_specs=specs, out_specs=outs
        ),
        compiler_params=pltpu.CompilerParams(vmem_limit_bytes=48 * 1024 * 1024),
        cost_estimate=pl.CostEstimate(
            flops=2 * rows * slots * width,
            bytes_accessed=2 * slots * width + 8 * rows * dim,
            transcendentals=0,
        ),
        name="combine",
    )(core, *args)


def shared_rows_kernel(rows, grads, weights, d_gate, d_up, hidden, out, back):
    def weight(number):
        part = weights[:, number]
        return part.reshape(part.shape[0] * part.shape[1], part.shape[2])

    gate_pre = matmul(rows[...], weight(0))
    up_pre = matmul(rows[...], weight(1))
    down_back = matmul(grads[...], weight(2))
    sigmoid_v = 0.5 + 0.5 * jnp.tanh(0.5 * gate_pre)
    silu_gate = gate_pre * sigmoid_v
    hidden_part = (silu_gate * up_pre).astype(bf16)
    hidden[...] = hidden_part
    out[...] = contract_last(hidden_part, weight(2)).astype(bf16)
    gate_part = (
        down_back * up_pre * (sigmoid_v * (1.0 + gate_pre * (1.0 - sigmoid_v)))
    ).astype(bf16)
    up_part = (down_back * silu_gate).astype(bf16)
    d_gate[...] = gate_part
    d_up[...] = up_part
    back[...] = (contract_last(gate_part, weight(0)) + contract_last(up_part, weight(1))).astype(
        bf16
    )


def shared_rows(rows, grads, weights, steps=2):
    count, dim = rows.shape
    hidden = weights.shape[3]
    wide = pl.BlockSpec((count // steps, dim), lambda i: (i, 0))
    narrow = pl.BlockSpec((count // steps, hidden), lambda i: (i, 0))
    shape = lambda columns: jax.ShapeDtypeStruct((count, columns), bf16)
    return pl.pallas_call(
        shared_rows_kernel,
        out_shape=[shape(hidden)] * 3 + [shape(dim)] * 2,
        grid=(steps,),
        in_specs=[wide, wide, pl.BlockSpec(weights.shape, lambda i: (0, 0, 0, 0))],
        out_specs=[narrow] * 3 + [wide] * 2,
        compiler_params=pltpu.CompilerParams(vmem_limit_bytes=56 * 1024 * 1024),
        cost_estimate=pl.CostEstimate(
            flops=12 * count * dim * hidden,
            bytes_accessed=6 * dim * hidden + 8 * count * dim,
            transcendentals=count * hidden,
        ),
        name="shared_rows",
    )(rows, grads, weights)


def shared_grads_kernel(rows, grads, d_gate, d_up, hidden, out):
    number = pl.program_id(0)

    def write(left, right):
        out[...] = contract_first(left[...], right[...]).astype(bf16).reshape(out.shape)

    pl.when(number == 0)(lambda: write(rows, d_gate))
    pl.when(number == 1)(lambda: write(rows, d_up))
    pl.when(number == 2)(lambda: write(grads, hidden))


def shared_grads(rows, grads, d_gate, d_up, hidden, own_rows):
    count, dim = rows.shape
    width = d_gate.shape[1]
    wide = pl.BlockSpec((count, dim), lambda i: (0, 0))
    narrow = pl.BlockSpec((count, width), lambda i: (0, 0))
    return pl.pallas_call(
        shared_grads_kernel,
        out_shape=jax.ShapeDtypeStruct((FSDP, 3, own_rows, width), bf16),
        grid=(3,),
        in_specs=[wide] * 2 + [narrow] * 3,
        out_specs=pl.BlockSpec((FSDP, 1, own_rows, width), lambda i: (0, i, 0, 0)),
        compiler_params=pltpu.CompilerParams(vmem_limit_bytes=48 * 1024 * 1024),
        cost_estimate=pl.CostEstimate(
            flops=6 * count * dim * width,
            bytes_accessed=6 * dim * width + 4 * count * dim,
            transcendentals=0,
        ),
        name="shared_grads",
    )(rows, grads, d_gate, d_up, hidden)


def attention_grads_kernel(spot, d_att, attended, rows, logits, gains, gain_lane, h_attn, d_qkv, *refs):
    for_z, for_y, whole = refs[:NZ], refs[NZ : NZ + NY], refs[-1]
    wide = attended.shape[1]

    def put(start, value):
        shape = (*whole.shape[:-1], value.shape[1])
        whole[..., start : start + value.shape[1]] = value.astype(bf16).reshape(shape)

    put(0, contract_first(d_att[...], attended[...]))
    put(wide, contract_first(rows[...], logits[...]) + contract_first(gains[...], gain_lane[...]))
    put(wide + LANES, contract_first(h_attn[...], d_qkv[...]))
    write_pieces(spot, whole, 0, for_z, for_y)


def attention_grads(spot, *args):
    d_att, attended, d_qkv = args[0], args[1], args[-1]
    count, dim = d_att.shape
    half = dim // FSDP // 2
    width = attended.shape[1] + LANES + d_qkv.shape[1]
    shapes = piece_shapes(1, half, width)
    outs = pl.pallas_call(
        attention_grads_kernel,
        out_shape=shapes,
        in_specs=[pl.BlockSpec(memory_space=pltpu.SMEM)]
        + [pl.BlockSpec(memory_space=pltpu.VMEM)] * len(args),
        out_specs=[pl.BlockSpec(memory_space=pltpu.VMEM)] * len(shapes),
        scratch_shapes=[pltpu.VMEM((NZ, NX, NY, 2, half, width), bf16)],
        compiler_params=pltpu.CompilerParams(vmem_limit_bytes=48 * 1024 * 1024),
        cost_estimate=pl.CostEstimate(
            flops=2 * count * dim * width,
            bytes_accessed=2 * dim * width + 8 * count * dim,
            transcendentals=0,
        ),
        name="attention_grads",
    )(spot, *args)
    return outs[:NZ], outs[NZ:]


def expert_grads_kernel(core, rows_own, rows_far, grads_own, grads_far, d_gate, d_up, scaled, *outs):
    half = pl.program_id(0)

    def write(rows, grads):
        outs[0][...] = contract_first(d_gate[...], rows[...])
        outs[1][...] = contract_first(d_up[...], rows[...])
        outs[2][...] = contract_first(scaled[...], grads[...])

    pl.when(half == 0)(lambda: write(rows_own, grads_own))
    pl.when(half == 1)(lambda: write(rows_far, grads_far))


def expert_grads(core, rows_own, rows_far, grads_own, grads_far, d_gate, d_up, scaled):
    rows, wide = grads_own.shape
    hidden = d_gate.shape[1]
    full = pl.BlockSpec((rows, wide), lambda h, c: (0, 0))
    part = pl.BlockSpec((rows, hidden), lambda h, c: (0, 0))
    result = pl.BlockSpec((hidden, wide), lambda h, c: (0, jnp.bitwise_xor(h, c[0])))
    return pl.pallas_call(
        expert_grads_kernel,
        out_shape=[jax.ShapeDtypeStruct((hidden, 2 * wide), f32)] * 3,
        grid_spec=pltpu.PrefetchScalarGridSpec(
            num_scalar_prefetch=1,
            grid=(2,),
            in_specs=[full] * 4 + [part] * 3,
            out_specs=[result] * 3,
        ),
        compiler_params=pltpu.CompilerParams(vmem_limit_bytes=56 * 1024 * 1024),
        cost_estimate=pl.CostEstimate(
            flops=12 * rows * wide * hidden,
            bytes_accessed=24 * hidden * wide + 12 * rows * wide,
            transcendentals=0,
        ),
        name="expert_grads",
    )(core, rows_own, rows_far, grads_own, grads_far, d_gate, d_up, scaled)


def per_device(
    tokens,
    g_attn,
    query_matrix,
    key_matrix,
    value_matrix,
    w_out,
    g_ffn,
    w_router,
    shared_gate,
    shared_up,
    shared_down,
    expert_gate,
    expert_up,
    expert_down,
    lengths,
    routes,
    cotangent,
):
    tok_dev, dim = tokens.shape
    group_rows = tok_dev * TP
    near = group_rows // 2
    experts = w_router.shape[1]
    own_rows = w_router.shape[0]
    q_width, kv_width = query_matrix.shape[1], key_matrix.shape[1]
    qkv_width = q_width + 2 * kv_width
    heads = q_width // HEAD_SIZE
    local_experts, _, hidden_own = expert_gate.shape
    half_dim = dim // 2
    fsdp_at = lax.axis_index("fsdp")
    rank = lax.axis_index("tp")
    core = lax.rem(rank, 2)
    core_vec = core.astype(jnp.int32).reshape(1)
    spot = jnp.stack(
        [fsdp_at // (NX * NY), lax.rem(fsdp_at // NY, NX), lax.rem(fsdp_at, NY)]
    ).astype(jnp.int32)

    route_blocks = routes.reshape(TP, tok_dev, routes.shape[1])
    own_routes = jnp.concatenate(
        [pick(route_blocks, jnp.bitwise_xor(b, rank), 0) for b in BLOCK_ORDER], axis=0
    )
    places = jnp.concatenate(
        [jnp.bitwise_xor(b, rank) * tok_dev + jnp.arange(tok_dev) for b in BLOCK_ORDER]
    ).astype(jnp.int32)
    expert_lane = jnp.arange(LANES, dtype=jnp.int32)[None, :]
    hot = (own_routes[:, 0:1] == expert_lane) | (own_routes[:, 1:2] == expert_lane)
    before = (places[None, :] < places[:, None]).astype(bf16)
    earlier = matmul(before, hot.astype(bf16))
    slots = experts * CAP
    slot_ids = jnp.arange(slots, dtype=jnp.int32)
    spread = (slot_ids[None, :] // CAP == jnp.arange(LANES, dtype=jnp.int32)[:, None]).astype(bf16)
    slot_wanted = matmul(jnp.where(hot, earlier, -1.0).astype(bf16), spread)
    dispatch = (slot_wanted == (slot_ids % CAP).astype(f32)[None, :]).astype(bf16)

    def core_half(values):
        return lax.dynamic_slice_in_dim(values, core * half_dim, half_dim, 1)

    small_tile = jnp.concatenate(
        [
            w_router,
            g_attn[:, None],
            g_ffn[:, None],
            jnp.zeros((own_rows, LANES - experts - 2), bf16),
        ],
        axis=1,
    )
    qkv_own = jnp.concatenate([query_matrix, key_matrix, value_matrix], axis=1)
    pair = gather_pair(jnp.concatenate([qkv_own, small_tile, w_out], axis=1)[None])
    grad_other = move_tp(cotangent, 2)
    *lines, grad_other = lax.optimization_barrier((*gather_lines(pair), grad_other))
    grad_pair = jnp.concatenate([cotangent, grad_other], axis=0)
    near_lines = gather_near(lines)
    grad_rows = jnp.concatenate([grad_pair, move_tp(grad_pair, 1)], axis=0)
    token_pair = jnp.concatenate([tokens, after(move_tp(tokens, 2), *near_lines)], axis=0)
    token_rows = jnp.concatenate([token_pair, move_tp(token_pair, 1)], axis=0)
    w_qkv, w_tile, w_out_all = gather_all(
        lines,
        near_lines,
        spot,
        (
            (0, 0, qkv_width),
            (0, qkv_width, LANES),
            (0, qkv_width + LANES, q_width),
        ),
    )
    slot_grads = contract_first(dispatch, core_half(grad_rows)).astype(bf16)
    grads_own = swap_fsdp(after(slot_grads, w_tile))
    shared_own = jnp.concatenate([shared_gate, shared_up, shared_down], axis=0)
    w_shared = lax.all_gather(
        shared_own, "fsdp", axis=0, tiled=True
    ).reshape(FSDP, 3, own_rows, shared_gate.shape[1])
    lane = lax.broadcasted_iota(jnp.int32, (8, LANES), 1)
    gain_pick = (lane == experts + lax.broadcasted_iota(jnp.int32, (8, LANES), 0)).astype(bf16)
    gains = contract_last(gain_pick, w_tile)
    gain_one, gain_two = gains[0:1], gains[1:2]

    hidden_all = local_experts * hidden_own

    def by_hidden(weights):
        return jnp.swapaxes(weights, 1, 2).reshape(hidden_all, dim)

    gate_w, up_w, down_w = by_hidden(expert_gate), by_hidden(expert_up), by_hidden(expert_down)

    ends = jnp.cumsum(lengths[0])
    where = jnp.stack([rank.astype(jnp.int32), ends[0], ends[1]]).astype(jnp.int32)
    normed_one, _ = norm_rows(token_rows.astype(f32), gain_one)
    h_attn = normed_one.astype(bf16)
    qkv = matmul(h_attn, w_qkv).astype(bf16)
    attended = attend(where, qkv, heads)
    attn_far = after(contract_last(attended[near:], w_out_all).astype(bf16), grads_own)
    attn_own = sum_chips(sum_cores(contract_last(attended[:near], w_out_all), attn_far))
    own_tokens = tokens.astype(f32)
    middle = own_tokens + attn_own
    normed_two, factor_two = norm_rows(middle, gain_two)
    h_ffn = gather_tp(normed_two.astype(bf16))

    logits = matmul(h_ffn, w_tile)
    top = jnp.max(jnp.where(hot, logits, -1e30), axis=-1, keepdims=True)
    gate_exp = jnp.where(hot, jnp.exp(jnp.minimum(logits - top, 0.0)), 0.0)
    gates = gate_exp / jnp.sum(gate_exp, axis=-1, keepdims=True)
    gate_high = gates.astype(bf16)
    gate_low = (gates - gate_high.astype(f32)).astype(bf16)
    gate_lanes = jnp.concatenate([gate_high[:, :experts], gate_low[:, :experts]], axis=1)

    slot_rows = contract_first(
        dispatch, jnp.concatenate([core_half(h_ffn), gate_lanes], axis=1)
    ).astype(bf16)
    grads_far = move_tp(after(grads_own, slot_rows), 1)
    rows_own = swap_fsdp(slot_rows)

    h_then = after(h_ffn, slot_rows)
    s_d_gate, s_d_up, s_hidden, shared_out, shared_back = shared_rows(h_then, grad_rows, w_shared)
    shared_parts = shared_grads(h_then, grad_rows, s_d_gate, s_d_up, s_hidden, own_rows)
    shared_lines = sum_along_z(shared_parts)

    rows_own = after(rows_own, shared_back, shared_parts)

    rows_far = move_tp(rows_own, 1)
    scal = jnp.stack([core.astype(jnp.int32), local_experts * fsdp_at.astype(jnp.int32)])
    d_gate, d_up, hidden, sent_far, dot_lanes = expert_rows(
        scal, rows_own, rows_far, grads_own, grads_far, gate_w, up_w, down_w
    )
    sent_far = move_tp(sent_far, 1)
    sent_own = (matmul(d_gate, core_half(gate_w)) + matmul(d_up, core_half(up_w))).astype(bf16)
    payload = add_and_join(sent_own, sent_far, dot_lanes)
    returned = swap_fsdp(payload)

    hidden_then = after(hidden, payload)
    grad_egate, grad_eup, grad_edown = expert_grads(
        core_vec, rows_own, rows_far, grads_own, grads_far, d_gate, d_up, hidden_then
    )
    down_own = core_half(down_w)
    down_far = lax.dynamic_slice_in_dim(down_w, (1 - core) * half_dim, half_dim, 1)
    out_far = move_tp(matmul(hidden_then, down_far).astype(bf16), 1)
    out_own = (matmul(hidden_then, down_own) + out_far.astype(f32)).astype(bf16)

    def expert_layout(grads):
        return jnp.swapaxes(grads.reshape(local_experts, hidden_own, dim), 1, 2)

    returned = after(returned, out_own, grad_egate)
    ffn_far, logits_far = combine(
        core_vec, 1, dispatch, returned, shared_back, bf16, gates, w_tile
    )
    ffn_near, logits_near = combine(
        core_vec, 0, dispatch, returned, shared_back, f32, gates, w_tile
    )
    d_h_ffn = sum_chips(sum_cores(ffn_near, ffn_far))
    d_middle = cotangent.astype(f32) + norm_back(middle, factor_two, gain_two, d_h_ffn)
    lane_ids = lax.broadcasted_iota(jnp.int32, (1, LANES), 1)
    gain_terms = (d_h_ffn * middle * factor_two).astype(bf16)
    gain_lane = jnp.broadcast_to(lane_ids == experts, (tok_dev, LANES)).astype(bf16)
    d_att_own = d_middle.astype(bf16)
    d_att_near = jnp.concatenate([d_att_own, move_tp(d_att_own, 2)], axis=0)
    out_back = swap_fsdp(after(out_own, d_att_near))
    d_att = jnp.concatenate([d_att_near, move_tp(d_att_near, 1)], axis=0)

    d_attended = matmul(after(d_att, shared_lines), w_out_all).astype(bf16)
    d_qkv = attend_back(where, qkv, d_attended, heads)
    grad_pieces = attention_grads(
        spot,
        d_att,
        attended,
        h_ffn,
        jnp.concatenate([logits_near, logits_far], axis=0),
        gain_terms,
        gain_lane,
        h_attn,
        d_qkv,
    )
    grad_received = trade_pieces(grad_pieces)
    sum_parts = add_pieces(grad_pieces[0][0], grad_pieces[1][0], grad_received)
    first_part = grad_received[0][0]
    d_qkv_then = after(d_qkv, first_part)
    attn_far = contract_last(d_qkv_then[near:], w_qkv).astype(bf16)
    d_h_half = sum_cores(contract_last(d_qkv_then[:near], w_qkv), attn_far)
    back_then = after(out_back, first_part)
    (out_far,) = combine(core_vec, 1, dispatch, back_then, shared_out, bf16)
    (out_near,) = combine(core_vec, 0, dispatch, back_then, shared_out, f32)
    out_half = sum_cores(out_near, out_far)
    shared_sums = sum_across(after(shared_lines, first_part))
    sum_parts = lax.optimization_barrier((*sum_parts, d_h_half, out_half))[:2]
    d_h_attn = sum_chips(d_h_half)
    output = (middle + sum_chips(out_half)).astype(bf16)
    sums = scatter_fsdp_two(sum_parts, spot)[0]
    out_sums, qkv_sums = sums[:, :q_width], sums[:, q_width + LANES :]
    gain_sum = jnp.sum(qkv_sums * qkv_own.astype(f32), axis=1, keepdims=True)
    tile_sums = small_sum_tp(
        sums[:, q_width : q_width + LANES] + jnp.where(lane_ids == experts + 1, gain_sum, 0.0)
    )
    _, factor_one = norm_rows(own_tokens, gain_one)
    grad_tokens = (d_middle + norm_back(own_tokens, factor_one, gain_one, d_h_attn)).astype(bf16)
    grad_g_attn = tile_sums[:, experts + 1] / g_attn.astype(f32)
    return (
        output,
        grad_tokens,
        grad_g_attn,
        qkv_sums[:, :q_width],
        qkv_sums[:, q_width : q_width + kv_width],
        qkv_sums[:, q_width + kv_width :],
        out_sums,
        tile_sums[:, experts],
        tile_sums[:, :experts],
        shared_sums[0],
        shared_sums[1],
        shared_sums[2],
        expert_layout(grad_egate),
        expert_layout(grad_eup),
        expert_layout(grad_edown),
    )


def solution(mesh):
    in_specs = (
        P(("fsdp", "tp"), None),
        P("fsdp"),
        P("fsdp", "tp"),
        P("fsdp", "tp"),
        P("fsdp", "tp"),
        P("fsdp", "tp"),
        P("fsdp"),
        P("fsdp", None),
        P("fsdp", "tp"),
        P("fsdp", "tp"),
        P("fsdp", "tp"),
        P("fsdp", None, "tp"),
        P("fsdp", None, "tp"),
        P("fsdp", None, "tp"),
        P("fsdp", None),
        P("fsdp", None),
        P(("fsdp", "tp"), None),
    )
    out_specs = (
        P(("fsdp", "tp"), None),
        P(("fsdp", "tp"), None),
        P("fsdp"),
        P("fsdp", "tp"),
        P("fsdp", "tp"),
        P("fsdp", "tp"),
        P("fsdp", "tp"),
        P("fsdp"),
        P("fsdp", None),
        P("fsdp", "tp"),
        P("fsdp", "tp"),
        P("fsdp", "tp"),
        P("fsdp", None, "tp"),
        P("fsdp", None, "tp"),
        P("fsdp", None, "tp"),
    )
    return jax.shard_map(
        per_device, mesh=mesh, in_specs=in_specs, out_specs=out_specs, check_vma=False
    )
```
